32 devices in a mesh: dp: 8 (over z, y), head: 4 (over x, core).
Axes of the slice: x: 2, y: 2, z: 4, core: 2. Of those that a mesh axis runs over, the one named last changes fastest.
Arguments:
- tokens: bfloat16 [24, 1024, 768], P('dp', 'head'), may hold values from -6 to 6
- lengths: int32 [24, 3], P('dp'), may hold values from 0 to 1024, as said below
- w_qkv: bfloat16 [768, 2304], replicated, may hold values from -0.21875 to 0.21875
- b_qkv: bfloat16 [2304], replicated, may hold values from -3 to 3
- w_out: bfloat16 [768, 768], replicated, may hold values from -1.25 to 1.25
- b_out: bfloat16 [768], replicated, may hold values from -2 to 2
- w_in: bfloat16 [768, 3072], replicated, may hold values from -0.21875 to 0.21875
- b_in: bfloat16 [3072], replicated, may hold values from -3 to 3
- w_down: bfloat16 [3072, 768], replicated, may hold values from -0.109375 to 0.109375
- b_down: bfloat16 [768], replicated, may hold values from -2 to 2
- norm1_gain: bfloat16 [768], replicated, may hold values from 0.099609375 to 1.8984375
- norm1_bias: bfloat16 [768], replicated, may hold values from -2 to 2
- norm2_gain: bfloat16 [768], replicated, may hold values from 0.099609375 to 1.8984375
- norm2_bias: bfloat16 [768], replicated, may hold values from -2 to 2
- cotangent: bfloat16 [24, 1024, 768], P('dp', 'head'), may hold values from -6 to 6
Outputs:
- output: bfloat16 [24, 1024, 768], P('dp', 'head')
- grad_tokens: bfloat16 [24, 1024, 768], P('dp', 'head')
- grad_w_qkv: float32 [768, 2304], replicated
- grad_b_qkv: float32 [2304], replicated
- grad_w_out: float32 [768, 768], replicated
- grad_b_out: float32 [768], replicated
- grad_w_in: float32 [768, 3072], replicated
- grad_b_in: float32 [3072], replicated
- grad_w_down: float32 [3072, 768], replicated
- grad_b_down: float32 [768], replicated
- grad_norm1_gain: float32 [768], replicated
- grad_norm1_bias: float32 [768], replicated
- grad_norm2_gain: float32 [768], replicated
- grad_norm2_bias: float32 [768], replicated
The draws below stay inside these ranges and needn't reach their ends.
Inputs may be any that keep to these rules, and one draw needn't show every extreme that they name: `lengths`: each row holds three slots (a sequence before, a main one, a sequence after); a side slot is 0 or from 32 to 127; the three sum to 1024.
All inputs are finite; a program needn't handle non-finite values.
Results may differ from the reference program's by a relative error of at most 0.0099.
Values may be sent and summed in bfloat16 or wider, within the bound.
No kernel may reach another device: no remote copies, remote signals or barrier semaphores. Data moves between devices by JAX's collectives and lax.ppermute only.
A program may use at most 192 MiB of HBM per device.

```python
import math
import jax
import jax.numpy as jnp
from jax import lax

D = 768
HEADS = 12
FF = 3072
ROW_LEN = 1024
ROWS = 24


def draw_lengths(key, part):
    key = jax.random.fold_in(key, 7)
    keys_list = jax.random.split(key, 4)
    shortest = ROW_LEN // 32
    bound_side = ROW_LEN // 8
    before = jax.random.randint(keys_list[0], (ROWS,), shortest, bound_side)
    after = jax.random.randint(keys_list[1], (ROWS,), shortest, bound_side)
    use_before = jax.random.randint(keys_list[2], (ROWS,), 0, 2)
    use_after = jax.random.randint(keys_list[3], (ROWS,), 0, 2)
    not_first = (jnp.arange(ROWS) > 0).astype(jnp.int32)
    before = before * use_before * not_first
    after = after * use_after * not_first
    middle = ROW_LEN - before - after
    return jnp.stack([before, middle, after], axis=1).astype(jnp.int32)


def block_levels(key, shape, cuts, least, top_value):
    gain, own = 1.0, jax.random.fold_in(key, 6)
    for dim, blocks in cuts:
        steps = jnp.exp(jax.random.uniform(jax.random.fold_in(own, dim), (blocks,), jnp.float32, least / len(cuts), top_value / len(cuts)))
        gain = gain * jnp.repeat(steps, shape[dim] // blocks).reshape([-1 if axis == dim else 1 for axis in range(len(shape))])
    return gain


def centred(own_key, shape, scale, most, shards=(), kind=jnp.bfloat16):
    loudness = block_levels(own_key, shape, shards, -0.22, 0.18) if shards else 1.0
    array = jax.random.normal(own_key, shape, jnp.float32) * scale * loudness
    return jnp.minimum(jnp.maximum(array, -most), most).astype(kind)


def setup_inputs(seed: int = 0) -> dict:
    key_of = jax.random.split(jax.random.key(seed), 16)
    return {
        "tokens": centred(key_of[0], (ROWS, ROW_LEN, D), 1.0, 6.0, ((0, 8), (1, 4))),
        "lengths": draw_lengths(jax.random.fold_in(key_of[15], 71), 0),
        "w_qkv": centred(key_of[2], (D, 3 * D), D ** -0.5, 0.21875),
        "b_qkv": centred(key_of[3], (3 * D,), 0.5, 3.0),
        "w_out": centred(key_of[4], (D, D), (D // 32) ** -0.5, 1.25),
        "b_out": centred(key_of[5], (D,), 0.3, 2.0),
        "w_in": centred(key_of[6], (D, FF), D ** -0.5, 0.21875),
        "b_in": centred(key_of[7], (FF,), 0.5, 3.0),
        "w_down": centred(key_of[8], (FF, D), FF ** -0.5, 0.109375),
        "b_down": centred(key_of[9], (D,), 0.3, 2.0),
        "norm1_gain": jnp.clip(1.0 + 0.18 * jax.random.normal(key_of[10], (D,), jnp.float32), 0.099609375, 1.8984375).astype(jnp.bfloat16),
        "norm1_bias": centred(key_of[11], (D,), 0.3, 2.0),
        "norm2_gain": jnp.clip(1.0 + 0.18 * jax.random.normal(key_of[12], (D,), jnp.float32), 0.099609375, 1.8984375).astype(jnp.bfloat16),
        "norm2_bias": centred(key_of[13], (D,), 0.3, 2.0),
        "cotangent": centred(key_of[14], (ROWS, ROW_LEN, D), 1.0, 6.0, ((0, 8), (1, 4))),
    }


highest = lax.Precision.HIGHEST

@jax.custom_vjp
def low(v):
    return lax.optimization_barrier(v.astype(jnp.bfloat16)).astype(jnp.float32)

@jax.custom_vjp
def low_back(v):
    return v

def low_keep(v):
    return (low(v), None)

def low_pass(kept, grad):
    return (grad,)

def back_keep(v):
    return (v, None)

def back_low(kept, grad):
    return (low(grad),)
low.defvjp(low_keep, low_pass)
low_back.defvjp(back_keep, back_low)

def layer_norm(values, gain_row, shift_row):
    center = values - lax.optimization_barrier(jnp.mean(values, axis=-1, keepdims=True))
    spread = lax.optimization_barrier(jnp.mean(center * center, axis=-1, keepdims=True))
    return center * lax.rsqrt(spread + 1e-05) * gain_row + shift_row

def matmul(left_mat, right_mat):
    flat_rows = left_mat.reshape(-1, left_mat.shape[-1])
    product = jnp.dot(flat_rows, right_mat, precision=highest, preferred_element_type=jnp.float32)
    return product.reshape(left_mat.shape[:-1] + (right_mat.shape[1],))

def rotary(values, places):
    rot_width = values.shape[-1] // 4
    half_width = rot_width // 2
    frequency = 1.0 / 10000.0 ** (jnp.arange(half_width, dtype=jnp.float32) * 2.0 / rot_width)
    angles = places[..., None] * frequency
    angles = jnp.concatenate([angles, angles], axis=-1)
    turned = values[..., :rot_width]
    swapped = jnp.concatenate([-turned[..., half_width:], turned[..., :half_width]], axis=-1)
    rotated = turned * jnp.cos(angles) + swapped * jnp.sin(angles)
    return jnp.concatenate([rotated, values[..., rot_width:]], axis=-1)

def segments(lengths, places):
    first_end = lengths[:, 0:1]
    second_end = first_end + lengths[:, 1:2]
    segment = (places[None, :] >= first_end).astype(jnp.int32) + (places[None, :] >= second_end).astype(jnp.int32)
    seg_start = jnp.where(segment == 0, 0, jnp.where(segment == 1, first_end, second_end))
    return (segment, places[None, :] - seg_start)

def attend_row(inputs):
    queries, key_mat, values, segment = inputs
    factor = 1.0 / math.sqrt(queries.shape[-1])
    scores = jnp.einsum('qhd,khd->hqk', queries, key_mat, precision=highest) * factor
    position = jnp.arange(segment.shape[0], dtype=jnp.int32)
    allowed = (segment[:, None] == segment[None, :]) & (position[None, :] <= position[:, None])
    scores = low_back(jnp.where(allowed[None], scores, -1000000000.0))
    row_top = lax.optimization_barrier(jnp.max(scores, axis=-1, keepdims=True))
    weights = jnp.exp(scores - row_top)
    weights = weights / lax.optimization_barrier(jnp.sum(weights, axis=-1, keepdims=True))
    return jnp.einsum('hqk,khd->qhd', low(weights), values, precision=highest)

def forward(resid_in, parameters, segment, offset):
    w_qkv, b_qkv, w_out, b_out, w_in, b_in, w_down, b_down, norm1_gain, norm1_bias, norm2_gain, norm2_bias = parameters
    row_count, row_len, model_width = resid_in.shape
    head_width = model_width // HEADS
    normed = low(layer_norm(resid_in, norm1_gain, norm1_bias))
    qkv_lin = low_back(matmul(normed, w_qkv) + b_qkv).reshape(row_count, row_len, HEADS, 3, head_width)
    angles_in = offset[:, :, None].astype(jnp.float32)
    queries = low_back(low(rotary(qkv_lin[:, :, :, 0], angles_in)))
    key_mat = low_back(low(rotary(qkv_lin[:, :, :, 1], angles_in)))
    values = low_back(low(qkv_lin[:, :, :, 2]))
    context_raw = lax.map(jax.checkpoint(attend_row), (queries, key_mat, values, segment))
    context = low_back(low(context_raw)).reshape(row_count, row_len, model_width)
    attn_out = matmul(context, w_out) + b_out
    hidden = low(layer_norm(resid_in, norm2_gain, norm2_bias))
    pre_act = low_back(matmul(hidden, w_in) + b_in)
    activated = low(jax.nn.gelu(pre_act, approximate=False))
    mlp_out = matmul(activated, w_down) + b_down
    return resid_in + attn_out + mlp_out

def reference(tokens, lengths, w_qkv, b_qkv, w_out, b_out, w_in, b_in, w_down, b_down, norm1_gain, norm1_bias, norm2_gain, norm2_bias, cotangent):
    places = jnp.arange(ROW_LEN, dtype=jnp.int32)
    segment, offset = segments(lengths, places)
    parameters = tuple((weight_arr.astype(jnp.float32) for weight_arr in (w_qkv, b_qkv, w_out, b_out, w_in, b_in, w_down, b_down, norm1_gain, norm1_bias, norm2_gain, norm2_bias)))

    def layer_fn(resid_in, weight_set):
        return forward(resid_in, weight_set, segment, offset)
    output, pullback = jax.vjp(layer_fn, tokens.astype(jnp.float32), parameters)
    grad_in, grad_set = pullback(cotangent.astype(jnp.float32))
    return (output.astype(jnp.bfloat16), grad_in.astype(jnp.bfloat16), grad_set[0], grad_set[1], grad_set[2], grad_set[3], grad_set[4], grad_set[5], grad_set[6], grad_set[7], grad_set[8], grad_set[9], grad_set[10], grad_set[11])
```

```python
import math, functools
import jax
import jax.numpy as jnp
from jax import lax
from jax.experimental import pallas as pl
from jax.experimental.pallas import tpu as pltpu

bf = jnp.bfloat16
f32 = jnp.float32
NN = (((1,), (0,)), ((), ()))
NT = (((1,), (1,)), ((), ()))
TN = (((0,), (0,)), ((), ()))


def mm(a, b, dims=NN):
    return lax.dot_general(a, b, dims, preferred_element_type=f32)


def norm_parts(x):
    center = x - jnp.mean(x, axis=-1, keepdims=True)
    rho = lax.rsqrt(jnp.mean(center * center, axis=-1, keepdims=True) + 1e-5)
    return center * rho, rho


def normal_cdf(x):
    bell = jnp.exp(-0.5 * x * x)
    t = 1.0 / (1.0 + (0.3275911 * math.sqrt(0.5)) * jnp.abs(x))
    poly = t * (0.127414796 + t * (-0.142248368 + t * (0.7107068705 + t * (-0.7265760135 + t * 0.5307027145))))
    tail = poly * bell
    return jnp.where(x >= 0, 1.0 - tail, tail), bell


def mlp_body(core_ref, x_ref, g_ref, wi_ref, wd_ref, bi_ref, gain_ref, bias_ref,
             out_ref, e_ref, gwi_ref, gwd_ref, gbi_ref, ln_ref,
             h_s, ht_s, gt_s, out_s, dh_s, gwi_s, gwd_s):
    j, i = pl.program_id(0), pl.program_id(1)
    nj, ni = pl.num_programs(0), pl.num_programs(1)
    gain = gain_ref[...].astype(f32)

    @pl.when(j == 0)
    def _():
        n, _ = norm_parts(x_ref[...].astype(f32))
        h = (n * gain + bias_ref[...].astype(f32)).astype(bf)
        h_s[i] = h
        ht_s[i] = h.T
        gt_s[i] = g_ref[...].T

    h = h_s[i]
    pre = mm(h, wi_ref[...]) + bi_ref[...].astype(f32)
    cdf, bell = normal_cdf(pre)
    act = (pre * cdf).astype(bf)
    slope = cdf + pre * bell * (1.0 / math.sqrt(2.0 * math.pi))
    d_act = mm(g_ref[...], wd_ref[...], NT)
    d_pre32 = d_act * slope
    d_pre = d_pre32.astype(bf)
    out = mm(act, wd_ref[...])
    dh = mm(d_pre, wi_ref[...], NT)
    gwi = mm(ht_s[i], d_pre)
    gwd = mm(gt_s[i], act)
    gbi = jnp.sum(d_pre.astype(f32), axis=0, keepdims=True)

    @pl.when(i == 0)
    def _():
        gwi_s[...] = gwi
        gwd_s[...] = gwd
        gbi_ref[...] = gbi

    @pl.when(i > 0)
    def _():
        gwi_s[...] += gwi
        gwd_s[...] += gwd
        gbi_ref[...] += gbi

    @pl.when(j == 0)
    def _():
        out_s[i] = out
        dh_s[i] = dh

    @pl.when(j > 0)
    def _():
        out_s[i] += out
        dh_s[i] += dh

    @pl.when(i == ni - 1)
    def _():
        gwi_ref[0] = gwi_s[...].astype(bf)
        gwd_ref[...] = gwd_s[...].astype(bf).T

    @pl.when(jnp.logical_and(j == nj - 1, i == 0))
    def _():
        ln_ref[...] = jnp.zeros_like(ln_ref)

    @pl.when(j == nj - 1)
    def _():
        d = dh_s[i]
        n, _ = norm_parts(x_ref[...].astype(f32))
        out_ref[...] = out_s[i].astype(bf)
        e_ref[...] = (d * gain).astype(bf)
        ln_ref[0:1, :] += jnp.sum(d * n, axis=0, keepdims=True)
        ln_ref[1:2, :] += jnp.sum(d, axis=0, keepdims=True)


def mlp(core, x, g, w_in, w_down, b_in, gain, bias, parts=2, tile=512, fft=768):
    toks, d = x.shape
    ff = w_in.shape[1] // parts
    nj, ni = ff // fft, toks // tile
    row = lambda v: v.reshape(1, -1)
    spec = pl.BlockSpec
    last = lambda j, i, c: (jnp.where(j == nj - 1, i, 0), 0)
    return pl.pallas_call(
        mlp_body,
        out_shape=(
            jax.ShapeDtypeStruct((toks, d), bf),
            jax.ShapeDtypeStruct((toks, d), bf),
            jax.ShapeDtypeStruct((nj, d, fft), bf),
            jax.ShapeDtypeStruct((ff, d), bf),
            jax.ShapeDtypeStruct((1, ff), f32),
            jax.ShapeDtypeStruct((8, d), f32),
        ),
        grid_spec=pltpu.PrefetchScalarGridSpec(
            num_scalar_prefetch=1,
            grid=(nj, ni),
            in_specs=[
                spec((tile, d), lambda j, i, c: (i, 0)),
                spec((tile, d), lambda j, i, c: (i, 0)),
                spec((d, fft), lambda j, i, c: (0, c[0] * nj + j)),
                spec((fft, d), lambda j, i, c: (c[0] * nj + j, 0)),
                spec((1, fft), lambda j, i, c: (0, c[0] * nj + j)),
                spec((1, d), lambda j, i, c: (0, 0)),
                spec((1, d), lambda j, i, c: (0, 0)),
            ],
            out_specs=[
                spec((tile, d), last),
                spec((tile, d), last),
                spec((1, d, fft), lambda j, i, c: (j, 0, 0)),
                spec((fft, d), lambda j, i, c: (j, 0)),
                spec((1, fft), lambda j, i, c: (0, j)),
                spec((8, d), lambda j, i, c: (0, 0)),
            ],
            scratch_shapes=[
                pltpu.VMEM((ni, tile, d), bf),
                pltpu.VMEM((ni, d, tile), bf),
                pltpu.VMEM((ni, d, tile), bf),
                pltpu.VMEM((ni, tile, d), f32),
                pltpu.VMEM((ni, tile, d), f32),
                pltpu.VMEM((d, fft), f32),
                pltpu.VMEM((d, fft), f32),
            ],
        ),
        compiler_params=pltpu.CompilerParams(vmem_limit_bytes=56 * 2**20),
        cost_estimate=pl.CostEstimate(flops=12 * toks * d * ff, bytes_accessed=30 * 2**20, transcendentals=toks * ff),
        name="mlp",
    )(core, x, g, w_in, w_down, row(b_in), row(gain), row(bias))


HW = 64
ROT = 16


def rope(u, cos, sin, back):
    t, width = u.shape
    lane = lax.broadcasted_iota(jnp.int32, (t, 128), 1)
    inner = lane % HW
    low = inner < ROT // 2
    outs = []
    for b in range(width // 128):
        v = u[:, b * 128:(b + 1) * 128]
        lo_rot, hi_rot = (2 * b) % 3 != 2, (2 * b + 1) % 3 != 2
        if (2 * b + 1) * HW >= 9 * HW:
            hi_rot = False
        if not (lo_rot or hi_rot):
            outs.append(v)
            continue
        turned = inner < ROT
        if not hi_rot:
            turned = turned & (lane < HW)
        if not lo_rot:
            turned = turned & (lane >= HW)
        up = pltpu.roll(v, 128 - ROT // 2, 1)
        down = pltpu.roll(v, ROT // 2, 1)
        if back:
            swapped = jnp.where(low, up, -down)
        else:
            swapped = jnp.where(low, -up, down)
        outs.append(jnp.where(turned, v * cos + swapped * sin, v))
    return jnp.concatenate(outs, axis=1)


def attn_body(x_ref, do_ref, w_ref, b_ref, gain_ref, bias_ref, cos_ref, sin_ref, start_ref,
              ctx_ref, e_ref, gw_ref, gb_ref, ln_ref,
              nb_s, n_s, q_s, k_s, v_s, do_s, o_s, dq_s, dk_s, dv_s, gw_s):
    r = pl.program_id(0)
    nr = pl.num_programs(0)
    row_len = x_ref.shape[1]
    nh = q_s.shape[0]
    ch = 256
    nch = row_len // ch
    gain = gain_ref[...].astype(f32)
    bias = bias_ref[...].astype(f32)

    @pl.when(r == 0)
    def _():
        gw_s[...] = jnp.zeros_like(gw_s)
        gb_ref[...] = jnp.zeros_like(gb_ref)
        ln_ref[...] = jnp.zeros_like(ln_ref)

    def project(ci, _):
        rows = pl.ds(pl.multiple_of(ci * ch, ch), ch)
        n, _ = norm_parts(x_ref[0, rows, :].astype(f32))
        n_s[rows, :] = n
        normed = (n * gain + bias).astype(bf)
        nb_s[rows, :] = normed
        lin = mm(normed, w_ref[...]) + b_ref[...].astype(f32)
        lin = rope(lin, cos_ref[0, rows, :], sin_ref[0, rows, :], False)
        for h in range(nh):
            q_s[h, rows, :] = (lin[:, h * 192:h * 192 + 64].astype(bf) * bf(0.125))
            k_s[h, rows, :] = lin[:, h * 192 + 64:h * 192 + 128].astype(bf)
            v_s[h, rows, :] = lin[:, h * 192 + 128:h * 192 + 192].astype(bf)
            do_s[h, rows, :] = do_ref[0, rows, h * 64:h * 64 + 64]
        return 0

    lax.fori_loop(0, nch, project, 0)

    def head(h, _):
        kt = k_s[h].T
        vt = v_s[h].T
        dot_ = do_s[h].astype(f32).T
        for qb in range(nch):
            kn = (qb + 1) * ch
            qs = slice(qb * ch, kn)
            q = q_s[h, qs, :]
            do = do_s[h, qs, :]
            st = mm(k_s[h, 0:kn, :], q, NT)
            kpos = lax.broadcasted_iota(jnp.int32, (kn, ch), 0)
            first = start_ref[0, :, qs]
            keep = kpos >= first
            qpos = lax.broadcasted_iota(jnp.int32, (kn, ch), 1) + qb * ch
            keep = keep & (kpos <= qpos)
            st = jnp.where(keep, st, -1e9)
            top = jnp.max(st, axis=0, keepdims=True)
            p = jnp.exp(st - top)
            p = p * (1.0 / jnp.sum(p, axis=0, keepdims=True))
            pb = p.astype(bf)
            ot = mm(vt[:, 0:kn], pb)
            delta = jnp.sum(ot * dot_[:, qs], axis=0, keepdims=True)
            dpt = mm(v_s[h, 0:kn, :], do, NT)
            ds = (p * (dpt - delta)).astype(bf)
            o_s[h, qs, :] = ot.T
            dq_s[h, qs, :] = mm(kt[:, 0:kn], ds).T * 0.125
            dv = mm(pb, do)
            dk = mm(ds, q)
            if qb:
                dv_s[h, 0:qb * ch, :] += dv[0:qb * ch]
                dk_s[h, 0:qb * ch, :] += dk[0:qb * ch]
            dv_s[h, qs, :] = dv[qb * ch:]
            dk_s[h, qs, :] = dk[qb * ch:]
        return 0

    lax.fori_loop(0, nh, head, 0)

    def back(ci, _):
        rows = pl.ds(pl.multiple_of(ci * ch, ch), ch)
        parts = []
        for h in range(nh):
            parts += [dq_s[h, rows, :], dk_s[h, rows, :], dv_s[h, rows, :]]
        parts.append(jnp.zeros((ch, 64), f32))
        d = jnp.concatenate(parts, axis=1).astype(bf).astype(f32)
        d = rope(d, cos_ref[0, rows, :], sin_ref[0, rows, :], True).astype(bf)
        gb_ref[...] += jnp.sum(d.astype(f32), axis=0, keepdims=True)
        dn = mm(d, w_ref[...], NT)
        n = n_s[rows, :]
        ln_ref[0:1, :] += jnp.sum(dn * n, axis=0, keepdims=True)
        ln_ref[1:2, :] += jnp.sum(dn, axis=0, keepdims=True)
        e_ref[0, rows, :] = (dn * gain).astype(bf)
        gw_s[...] += mm(d.T, nb_s[rows, :])
        ctx_ref[0, rows, :] = jnp.concatenate([o_s[h, rows, :] for h in range(nh)], axis=1).astype(bf)
        return 0

    lax.fori_loop(0, nch, back, 0)

    @pl.when(r == nr - 1)
    def _():
        gw_ref[...] = gw_s[0:gw_ref.shape[0], :].astype(bf)


def attention(x, do, w, b, gain, bias, cos, sin, start):
    rows, row_len, d = x.shape
    width = w.shape[1]
    nh = do.shape[2] // HW
    row = lambda v: v.reshape(1, -1)
    spec = pl.BlockSpec
    per_row = lambda *s: spec((1,) + s, lambda r: (r, 0, 0))
    whole = lambda *s: spec(s, lambda r: (0, 0))
    real = nh * 3 * HW
    return pl.pallas_call(
        attn_body,
        grid=(rows,),
        out_shape=(
            jax.ShapeDtypeStruct((rows, row_len, nh * HW), bf),
            jax.ShapeDtypeStruct((rows, row_len, d), bf),
            jax.ShapeDtypeStruct((real, d), bf),
            jax.ShapeDtypeStruct((1, width), f32),
            jax.ShapeDtypeStruct((8, d), f32),
        ),
        in_specs=[
            per_row(row_len, d), per_row(row_len, nh * HW), whole(d, width), whole(1, width),
            whole(1, d), whole(1, d), per_row(row_len, 128), per_row(row_len, 128), per_row(1, row_len),
        ],
        out_specs=[
            per_row(row_len, nh * HW), per_row(row_len, d), whole(real, d), whole(1, width), whole(8, d),
        ],
        scratch_shapes=[
            pltpu.VMEM((row_len, d), bf),
            pltpu.VMEM((row_len, d), f32),
            pltpu.VMEM((nh, row_len, HW), bf),
            pltpu.VMEM((nh, row_len, HW), bf),
            pltpu.VMEM((nh, row_len, HW), bf),
            pltpu.VMEM((nh, row_len, HW), bf),
            pltpu.VMEM((nh, row_len, HW), f32),
            pltpu.VMEM((nh, row_len, HW), f32),
            pltpu.VMEM((nh, row_len, HW), f32),
            pltpu.VMEM((nh, row_len, HW), f32),
            pltpu.VMEM((width, d), f32),
        ],
        compiler_params=pltpu.CompilerParams(vmem_limit_bytes=56 * 2**20),
        cost_estimate=pl.CostEstimate(flops=rows * row_len * (6 * d * real + 6 * row_len * nh * HW * 4), bytes_accessed=20 * 2**20, transcendentals=rows * nh * row_len * row_len // 2),
        name="attention",
    )(x, do, w, row(b), row(gain), row(bias), cos, sin, start)


from jax.sharding import PartitionSpec as P

HEADS = 12


def swap(x, axis, bit):
    n = lax.axis_size(axis)
    return lax.ppermute(x, axis, [(i, i ^ bit) for i in range(n)])


def pair(mine, other, bit, dim):
    first = jnp.where(bit == 0, mine, other)
    second = jnp.where(bit == 0, other, mine)
    return jnp.concatenate([first, second], axis=dim)


def rs_step(parts, axis, bit, mine):
    keep = lax.dynamic_index_in_dim(parts, mine, 0, False)
    send = lax.dynamic_index_in_dim(parts, 1 - mine, 0, False)
    return (keep.astype(f32) + swap(send, axis, bit).astype(f32)).astype(bf)


def rs_cross(parts, axis, count, step, mine):
    total = lax.dynamic_index_in_dim(parts, mine, 0, False).astype(f32)
    for k in range(1, count):
        total = total + swap(lax.dynamic_index_in_dim(parts, mine ^ k, 0, False), axis, step * k).astype(f32)
    return total.astype(bf)


def ag_step(x, axis, bit):
    return jnp.stack([x, swap(x, axis, bit)])


def ag_cross(x, axis, count, step):
    return jnp.stack([x] + [swap(x, axis, step * k) for k in range(1, count)])


def tables(lengths, row_len):
    pos = jnp.arange(row_len, dtype=jnp.int32)[None, :]
    first_end = lengths[:, 0:1]
    second_end = first_end + lengths[:, 1:2]
    start = jnp.where(pos < first_end, 0, jnp.where(pos < second_end, first_end, second_end))
    half = ROT // 2
    freq = 1.0 / 10000.0 ** (jnp.arange(half, dtype=f32) * 2.0 / ROT)
    angle = (pos - start)[:, None, :].astype(f32) * freq[None, :, None]

    def full(t):
        t = jnp.concatenate([t, t], axis=1)
        t = jnp.pad(t, ((0, 0), (0, HW - ROT), (0, 0)))
        return jnp.swapaxes(jnp.concatenate([t, t], axis=1), 1, 2)

    return full(jnp.cos(angle)), full(jnp.sin(angle)), start[:, None, :]


def fill_body(own_ref, pieces_ref, wi_ref, wd_ref):
    _, nc, ny, nz, nx, rows, d = pieces_ref.shape
    x, c, y, z = own_ref[0], own_ref[1], own_ref[2], own_ref[3]
    for jc in range(nc):
        for jx in range(nx):
            for jy in range(ny):
                for jz in range(nz):
                    at = ((y ^ jy) * nz + (z ^ jz)) * rows
                    block = ((c ^ jc) * nx + (x ^ jx))
                    wi_ref[pl.ds(pl.multiple_of(at, 8), rows), pl.ds(pl.multiple_of(block * d, 128), d)] = pieces_ref[0, jc, jy, jz, jx].astype(f32)
                    wd_ref[pl.ds(pl.multiple_of(block * d + at, 8), rows), :] = pieces_ref[1, jc, jy, jz, jx].astype(f32)


def fill_mlp(own, pieces):
    _, nc, ny, nz, nx, rows, d = pieces.shape
    vm = pl.BlockSpec(memory_space=pltpu.VMEM)
    return pl.pallas_call(
        fill_body,
        out_shape=(jax.ShapeDtypeStruct((d, nc * nx * d), f32), jax.ShapeDtypeStruct((nc * nx * d, d), f32)),
        in_specs=[pl.BlockSpec(memory_space=pltpu.SMEM), vm],
        out_specs=(vm, vm),
        compiler_params=pltpu.CompilerParams(vmem_limit_bytes=56 * 2**20),
        name="fill_mlp",
    )(own, pieces)


def fill_attn_body(own_ref, pieces_ref, wq_ref, wo_ref, s):
    nc, ny, nz, nx, rows, d = pieces_ref.shape
    x, c, y, z = own_ref[0], own_ref[1], own_ref[2], own_ref[3]
    real = wq_ref.shape[1] // (nc * nx)
    out_rows = wo_ref.shape[0] // (nc * nx)
    for jc in range(nc):
        for jx in range(nx):
            block = ((c ^ jc) * nx + (x ^ jx))
            for jy in range(ny):
                for jz in range(nz):
                    at = ((y ^ jy) * nz + (z ^ jz)) * rows
                    s[block, pl.ds(pl.multiple_of(at, 8), rows), :] = pieces_ref[jc, jy, jz, jx].astype(f32)
    for b in range(nc * nx):
        wq_ref[:, b * real:(b + 1) * real] = s[b, 0:real, :].T
        wo_ref[b * out_rows:(b + 1) * out_rows, :] = s[b, real:real + out_rows, :]


def fill_attn(own, pieces, real):
    nc, ny, nz, nx, rows, d = pieces.shape
    vm = pl.BlockSpec(memory_space=pltpu.VMEM)
    return pl.pallas_call(
        fill_attn_body,
        out_shape=(jax.ShapeDtypeStruct((d, nc * nx * real), f32), jax.ShapeDtypeStruct((d, d), f32)),
        in_specs=[pl.BlockSpec(memory_space=pltpu.SMEM), vm],
        out_specs=(vm, vm),
        scratch_shapes=[pltpu.VMEM((nc * nx, d, d), f32)],
        compiler_params=pltpu.CompilerParams(vmem_limit_bytes=56 * 2**20),
        name="fill_attn",
    )(own, pieces)


def on_device(tokens, lengths, w_qkv, b_qkv, w_out, b_out, w_in, b_in, w_down, b_down,
              norm1_gain, norm1_bias, norm2_gain, norm2_bias, cotangent):
    rows, span, d = tokens.shape
    ff = w_in.shape[1]
    head = lax.axis_index("head")
    dp = lax.axis_index("dp")
    x, c = head // 2, head % 2
    y, z = dp % 2, dp // 2
    nz = lax.axis_size("dp") // 2
    own = jnp.stack([x, c, y, z]).astype(jnp.int32)
    row_len = 4 * span
    lh = HEADS // 4
    hd = lh * HW

    tok2 = pair(tokens, swap(tokens, "head", 1), c, 1)
    g2 = pair(cotangent, swap(cotangent, "head", 1), c, 1)
    far = swap(tokens, "head", 2)
    far2 = pair(far, swap(far, "head", 1), c, 1)
    tok4 = pair(tok2, far2, x, 1)

    w_out_c = lax.dynamic_slice_in_dim(w_out, c * 2 * hd, 2 * hd, 0)
    at = (c * 2 + x) * (3 * hd)
    w_q = jnp.pad(lax.dynamic_slice_in_dim(w_qkv, at, 3 * hd, 1), ((0, 0), (0, HW)))
    b_q = jnp.pad(lax.dynamic_slice_in_dim(b_qkv, at, 3 * hd, 0), ((0, HW)))
    cos, sin, start = tables(lengths, row_len)

    g2f = g2.reshape(-1, d)
    dctx = mm(g2f, w_out_c, NT).astype(bf).reshape(rows, 2 * span, 2, hd)
    d_mine = lax.dynamic_index_in_dim(dctx, x, 2, False)
    d_far = swap(lax.dynamic_index_in_dim(dctx, 1 - x, 2, False), "head", 2)
    do4 = pair(d_mine, d_far, x, 1)

    m_out, m_e, gwi, gwd, gbi, ln2 = mlp(c[None], tok2.reshape(-1, d), g2f, w_in, w_down, b_in, norm2_gain, norm2_bias)
    ctx, e1, gq, gbq, ln1 = attention(tok4, do4, w_q, b_q, norm1_gain, norm1_bias, cos, sin, start)

    gm = jnp.stack([gwi, gwd.reshape(2, d, d)])
    gm = gm.reshape(2, 2, 2, nz, d // (2 * nz), d)
    gm = rs_step(jnp.moveaxis(gm, 2, 0), "dp", 1, y)
    gm = rs_cross(jnp.moveaxis(gm, 2, 0), "dp", nz, 2, z)
    gm = rs_step(jnp.moveaxis(gm, 1, 0), "head", 2, x)
    f = ag_step(gm, "head", 2)
    f = ag_cross(f, "dp", nz, 2)
    f = ag_step(f, "dp", 1)
    f = ag_step(f, "head", 1)
    grad_w_in, grad_w_down = fill_mlp(own, jnp.moveaxis(f, 4, 0))

    ctx_h = ctx.reshape(rows, 2, 2 * span, hd)
    c_mine = lax.dynamic_index_in_dim(ctx_h, x, 1, False)
    c_far = swap(lax.dynamic_index_in_dim(ctx_h, 1 - x, 1, False), "head", 2)
    ctx2 = pair(c_mine, c_far, x, 2).reshape(-1, 2 * hd)
    part = (mm(ctx2, w_out_c) + m_out.astype(f32)).astype(bf).reshape(rows, 2, span, d)
    gwo = mm(ctx2, g2f, TN).astype(bf).reshape(2, hd, d)
    total = rs_step(jnp.moveaxis(part, 1, 0), "head", 1, c).astype(f32)
    bias = (b_out.astype(f32) + b_down.astype(f32))
    output = (tokens.astype(f32) + total + bias).astype(bf)

    e1 = e1.reshape(rows, 2, 2, span, d)
    e2 = m_e.reshape(rows, 1, 2, span, d)
    here = (jnp.arange(2) == x).reshape(1, 2, 1, 1, 1)
    e = (e1.astype(f32) + jnp.where(here, e2.astype(f32), 0.0)).astype(bf)
    e = rs_step(jnp.moveaxis(e, 2, 0), "head", 1, c)
    e = rs_step(jnp.moveaxis(e, 1, 0), "head", 2, x).astype(f32)
    n, rho = norm_parts(tokens.astype(f32))
    dx = rho * (e - jnp.mean(e, -1, keepdims=True) - n * jnp.mean(e * n, -1, keepdims=True))
    grad_tokens = (cotangent.astype(f32) + dx).astype(bf)

    gwo = rs_step(gwo, "head", 2, x)
    ga = jnp.concatenate([gq, gwo], axis=0).reshape(2, nz, d // (2 * nz), d)
    ga = rs_step(ga, "dp", 1, y)
    ga = rs_cross(ga, "dp", nz, 2, z)
    f = ag_step(ga, "head", 2)
    f = ag_cross(f, "dp", nz, 2)
    f = ag_step(f, "dp", 1)
    f = ag_step(f, "head", 1)
    grad_w_qkv, grad_w_out = fill_attn(own, f, 3 * hd)

    gsum = jnp.sum(cotangent.astype(f32), axis=(0, 1))
    v_in = lax.dynamic_update_slice(jnp.zeros((ff,), f32), gbi[0], (c * (ff // 2),))
    v_q = lax.dynamic_update_slice(jnp.zeros((3 * d,), f32), gbq[0, :3 * hd], (at,))
    v = jnp.concatenate([v_in, v_q, gsum, ln1[0], ln1[1], ln2[0], ln2[1]]).reshape(-1, 128)
    for axis in ("head", "dp"):
        bit = 1
        while bit < lax.axis_size(axis):
            v = v + swap(v, axis, bit)
            bit *= 2
    v = v.reshape(-1)
    cut = lambda a, n: v[a:a + n]
    o = ff + 3 * d
    return (output, grad_tokens, grad_w_qkv, cut(ff, 3 * d), grad_w_out, cut(o, d), grad_w_in, cut(0, ff),
            grad_w_down, cut(o, d), cut(o + d, d), cut(o + 2 * d, d), cut(o + 3 * d, d), cut(o + 4 * d, d))


def solution(mesh):
    split = P("dp", "head", None)
    return jax.shard_map(
        on_device, mesh=mesh,
        in_specs=(split, P("dp", None)) + (P(),) * 12 + (split,),
        out_specs=(split, split) + (P(),) * 12,
        check_vma=False,
    )
```

```python
import math, functools
import jax
import jax.numpy as jnp
from jax import lax
from jax.experimental import pallas as pl
from jax.experimental.pallas import tpu as pltpu

bf = jnp.bfloat16
f32 = jnp.float32
NN = (((1,), (0,)), ((), ()))
NT = (((1,), (1,)), ((), ()))
TN = (((0,), (0,)), ((), ()))


def mm(a, b, dims=NN):
    return lax.dot_general(a, b, dims, preferred_element_type=f32)


def norm_parts(x):
    center = x - jnp.mean(x, axis=-1, keepdims=True)
    rho = lax.rsqrt(jnp.mean(center * center, axis=-1, keepdims=True) + 1e-5)
    return center * rho, rho


def normal_cdf(x):
    bell = jnp.exp(-0.5 * x * x)
    t = 1.0 / (1.0 + (0.3275911 * math.sqrt(0.5)) * jnp.abs(x))
    poly = t * (0.127414796 + t * (-0.142248368 + t * (0.7107068705 + t * (-0.7265760135 + t * 0.5307027145))))
    tail = poly * bell
    return jnp.where(x >= 0, 1.0 - tail, tail), bell


def put_quarters(acc, kind, refs, x, y, z):
    nz, rows = refs[0].shape[0], refs[0].shape[1]
    for hy in range(2):
        for at, ref in enumerate(refs):
            jx, jy = at // 2, at % 2

            @pl.when(((x ^ kind) == jx) & ((y ^ hy) == jy))
            def _():
                for hz in range(nz):
                    row = (hz * 2 + hy) * rows
                    ref[hz ^ z] = acc[row:row + rows, :].astype(bf)


def put_halves(acc, half, keep_ref, send_ref, y, z):
    nz, rows = keep_ref.shape[0], keep_ref.shape[1]
    for hy in range(2):
        for ref, stays in ((keep_ref, True), (send_ref, False)):
            @pl.when((y == hy) == stays)
            def _():
                for hz in range(nz):
                    at = hy * half + hz * rows
                    ref[hz ^ z] = acc[at:at + rows, :].astype(bf)


B_IN, B_QKV, B_LAST, GAIN1, BIAS1, GAIN2, BIAS2, VECS = 0, 4, 7, 8, 9, 10, 11, 16


def vector(vec_ref, k, d, count=1):
    return jnp.concatenate([vec_ref[pl.ds(k + i, 1), :] for i in range(count)], axis=1)


def mlp_body(first, own_ref, xo_ref, xp_ref, go_ref, gp_ref, wi_ref, wd_ref, vec_ref, *rest):
    if first:
        out_ref, dh_ref, g0_ref, g1_ref, g2_ref, g3_ref, gbi_ref, *rest = rest
    else:
        outp_ref, dhp_ref, out_ref, e_ref, g0_ref, g1_ref, g2_ref, g3_ref, gbi_ref, ln_ref, n_s, *rest = rest
    h_s, ht_s, g_s, gwi_s, gwd_s = rest
    i, ni = pl.program_id(0), pl.num_programs(0)
    d = xo_ref.shape[1]
    gain = vector(vec_ref, GAIN2, d)

    def start(x_ref, g_ref):
        n, _ = norm_parts(x_ref[...].astype(f32))
        h = (n * gain + vector(vec_ref, BIAS2, d)).astype(bf)
        if not first:
            n_s[...] = n
        h_s[...] = h
        ht_s[...] = h.T
        g_s[...] = g_ref[...]

    @pl.when(i == 0)
    def _():
        start(xo_ref, go_ref)

    @pl.when(i == 1)
    def _():
        start(xp_ref, gp_ref)

    unit = 0 if first else 1
    pre = mm(h_s[...], wi_ref[...]) + vector(vec_ref, B_IN + own_ref[1] * 2 + unit, d)
    d_act = mm(g_s[...], wd_ref[...], NT)
    cdf, bell = normal_cdf(pre)
    act = (pre * cdf).astype(bf)
    slope = cdf + pre * bell * (1.0 / math.sqrt(2.0 * math.pi))
    d_pre = (d_act * slope).astype(bf)
    out = mm(act, wd_ref[...])
    dh = mm(d_pre, wi_ref[...], NT)
    gwi = mm(ht_s[...], d_pre)
    gwd = mm(act.T, g_s[...])
    gbi = jnp.sum(d_pre.astype(f32), axis=0, keepdims=True)

    @pl.when(i == 0)
    def _():
        gwi_s[...] = gwi
        gwd_s[...] = gwd
        gbi_ref[0:1, :] = gbi
        gbi_ref[1:2, :] = jnp.sum(g_s[...].astype(f32), axis=0, keepdims=True)

    @pl.when(i == ni - 1)
    def _():
        gwi_s[...] += gwi
        gwd_s[...] += gwd
        gbi_ref[0:1, :] += gbi
        x, y, z = own_ref[0], own_ref[2], own_ref[3]
        gw = [g0_ref, g1_ref, g2_ref, g3_ref]
        put_quarters(gwi_s, 0, gw, x, y, z)
        put_quarters(gwd_s, 1, gw, x, y, z)

    if first:
        out_ref[...] = out.astype(bf)
        dh_ref[...] = dh.astype(bf)
    else:
        @pl.when(i == 0)
        def _():
            ln_ref[...] = jnp.zeros_like(ln_ref)

        dh = dh + dhp_ref[...].astype(f32)
        out_ref[...] = (out + outp_ref[...].astype(f32)).astype(bf)
        e_ref[...] = (dh * gain).astype(bf)
        ln_ref[0:1, :] += jnp.sum(dh * n_s[...], axis=0, keepdims=True)
        ln_ref[1:2, :] += jnp.sum(dh, axis=0, keepdims=True)


def mlp(own, unit, xo, xp, go, gp, w_in, w_down, vecs, nz, before=None):
    toks, d = xo.shape
    first = before is None
    rows = d // (2 * nz)
    spec = pl.BlockSpec
    once = lambda *s: spec(s, lambda i, o: (0,) * len(s), pipeline_mode=pl.Buffered(1))
    tile = spec((toks, d), lambda i, o: (i, 0))
    part = lambda o: o[1] * 2 + unit
    shape = jax.ShapeDtypeStruct
    vm = pltpu.VMEM
    ins = [once(toks, d)] * 4 + [spec((d, d), lambda i, o: (0, part(o)), pipeline_mode=pl.Buffered(1)),
                                 spec((d, d), lambda i, o: (part(o), 0), pipeline_mode=pl.Buffered(1)), once(*vecs.shape)]
    args = [own, xo, xp, go, gp, w_in, w_down, vecs]
    outs = [shape((2 * toks, d), bf), shape((2 * toks, d), bf)] + [shape((nz, rows, d), bf)] * 4 + [shape((8, d), f32)]
    ospecs = [tile, tile] + [once(nz, rows, d)] * 4 + [once(8, d)]
    scratch = [vm((toks, d), bf)] * 3 + [vm((d, d), f32)] * 2
    if not first:
        ins += [tile, tile]
        args += list(before)
        outs.append(shape((8, d), f32))
        ospecs.append(once(8, d))
        scratch = [vm((toks, d), f32)] + scratch
    return pl.pallas_call(
        functools.partial(mlp_body, first),
        out_shape=tuple(outs),
        grid_spec=pltpu.PrefetchScalarGridSpec(num_scalar_prefetch=1, grid=(2,), in_specs=ins, out_specs=ospecs, scratch_shapes=scratch),
        compiler_params=pltpu.CompilerParams(vmem_limit_bytes=60 * 2**20),
        cost_estimate=pl.CostEstimate(flops=24 * toks * d * d, bytes_accessed=20 * 2**20, transcendentals=2 * toks * d),
        name="mlp%d" % unit,
    )(*args)


HW = 64
ROT = 16


def rope(u, cos, sin, back):
    t, width = u.shape
    lane = lax.broadcasted_iota(jnp.int32, (t, 128), 1)
    inner = lane % HW
    low = inner < ROT // 2
    outs = []
    for b in range(width // 128):
        v = u[:, b * 128:(b + 1) * 128]
        lo_rot, hi_rot = (2 * b) % 3 != 2, (2 * b + 1) % 3 != 2
        if (2 * b + 1) * HW >= 9 * HW:
            hi_rot = False
        if not (lo_rot or hi_rot):
            outs.append(v)
            continue
        turned = inner < ROT
        if not hi_rot:
            turned = turned & (lane < HW)
        if not lo_rot:
            turned = turned & (lane >= HW)
        up = pltpu.roll(v, 128 - ROT // 2, 1)
        down = pltpu.roll(v, ROT // 2, 1)
        if back:
            swapped = jnp.where(low, up, -down)
        else:
            swapped = jnp.where(low, -up, down)
        outs.append(jnp.where(turned, v * cos + swapped * sin, v))
    return jnp.concatenate(outs, axis=1)


def attn_body(first, last, own_ref, xo_ref, xp_ref, xf_ref, xfp_ref, go_ref, gp_ref, gf_ref, gfp_ref, w0_ref, w1_ref, w2_ref, w3_ref, w4_ref, wo_ref, vec_ref,
              cos_ref, sin_ref, start_ref, me_ref, *rest):
    if not first:
        gwp_ref, gbp_ref, lnp_ref, *rest = rest
        rest = rest[4:]
    if last:
        gb0_ref, gb1_ref, ln2_ref, *rest = rest
    ctx_ref, ctxs_ref, e_ref, es_ref, *rest = rest
    if last:
        keep_ref, send_ref, v_ref, *scratch = rest
        gw_s, gb_ref, ln_ref = scratch[-3:]
    else:
        gw_s, gb_ref, ln_ref, *scratch = rest
    x_s, g_s, nb_s, q_s, k_s, v_s, do_s, o_s, dq_s, dk_s, dv_s, cs_s, b_ref, w_ref = scratch[:14]
    head_at = own_ref[0] * 2 + own_ref[1]
    ch = xo_ref.shape[1]
    row_len = start_ref.shape[2]
    nh = q_s.shape[0]
    nch = row_len // ch
    real = nh * 3 * HW
    d_model = x_s.shape[2]
    gain = vector(vec_ref, GAIN1, d_model)
    bias = vector(vec_ref, BIAS1, d_model)

    @pl.when(pl.program_id(0) == 0)
    def _():
        block = own_ref[1] * 2 + own_ref[0]
        b_ref[...] = jnp.zeros_like(b_ref)
        columns = vector(vec_ref, B_QKV, d_model, 3)
        for b in range(4):
            @pl.when(block == b)
            def _():
                b_ref[:, 0:real] = columns[:, b * real:(b + 1) * real]
        for k, ref in enumerate((w0_ref, w1_ref, w2_ref, w3_ref, w4_ref)):
            w_ref[:, k * 128:(k + 1) * 128] = ref[...]
        if first:
            gw_s[...] = jnp.zeros_like(gw_s)
            gb_ref[...] = jnp.zeros_like(gb_ref)
            ln_ref[...] = jnp.zeros_like(ln_ref)
        else:
            gw_s[...] = gwp_ref[...]
            gb_ref[...] = gbp_ref[...]
            ln_ref[...] = lnp_ref[...]

    width = w_ref.shape[1]
    odd = own_ref[0]
    back_by = (width - HW) * odd
    for t, (ref, rest_value) in enumerate(((cos_ref, 1.0), (sin_ref, 0.0))):
        one = ref[0]
        still = jnp.full((HW - ROT, row_len), rest_value, f32)
        cs_s[t] = jnp.concatenate([one, one, still, one, one, still], axis=0).T
    for p, (ref, ref2) in enumerate(((xo_ref, go_ref), (xp_ref, gp_ref), (xf_ref, gf_ref), (xfp_ref, gfp_ref))):
        x_s[p] = ref[0]
        g_s[p] = ref2[0]

    def project(p, _):
        ci = p ^ head_at
        rows = pl.ds(pl.multiple_of(ci * ch, ch), ch)
        n, _ = norm_parts(x_s[p].astype(f32))
        normed = (n * gain + bias).astype(bf)
        nb_s[rows, :] = normed
        lin = pltpu.roll(mm(normed, w_ref[...]), back_by, 1) + b_ref[...]
        lin = rope(lin, cs_s[0, rows, :], cs_s[1, rows, :], False)
        for h in range(nh):
            q_s[h, rows, :] = (lin[:, h * 192:h * 192 + 64].astype(bf) * bf(0.125))
            k_s[h, rows, :] = lin[:, h * 192 + 64:h * 192 + 128].astype(bf)
            v_s[h, rows, :] = lin[:, h * 192 + 128:h * 192 + 192].astype(bf)
        d_ctx = mm(g_s[p], wo_ref[...], NT).astype(bf)
        for h in range(nh):
            do_s[h, rows, :] = d_ctx[:, h * HW:(h + 1) * HW]
        return 0

    for p in range(nch):
        project(p, 0)
    def head(h, _):
        kt = k_s[h].T
        vt = v_s[h].T
        dot_ = do_s[h].astype(f32).T
        for qb in range(nch):
            k0, kn = qb * ch, (qb + 1) * ch
            qs = slice(k0, kn)
            q = q_s[h, qs, :]
            do = do_s[h, qs, :]
            first = start_ref[0, :, qs]
            kpos = lax.broadcasted_iota(jnp.int32, (ch, ch), 0)
            qpos = lax.broadcasted_iota(jnp.int32, (ch, ch), 1)
            st = []
            top = None
            for kb in range(qb + 1):
                s = mm(k_s[h, kb * ch:(kb + 1) * ch, :], q, NT)
                keep = kpos >= first - kb * ch
                if kb == qb:
                    keep = keep & (kpos <= qpos)
                s = jnp.where(keep, s, -1e9)
                m = jnp.max(s, axis=0, keepdims=True)
                top = m if top is None else jnp.maximum(top, m)
                st.append(s)
            size = None
            for kb in range(qb + 1):
                st[kb] = jnp.exp(st[kb] - top)
                m = jnp.sum(st[kb], axis=0, keepdims=True)
                size = m if size is None else size + m
            inv = 1.0 / size
            ot = None
            for kb in range(qb + 1):
                ks = slice(kb * ch, (kb + 1) * ch)
                st[kb] = st[kb] * inv
                pb = st[kb].astype(bf)
                o = mm(vt[:, ks], pb)
                ot = o if ot is None else ot + o
                dv = mm(pb, do)
                if kb < qb:
                    dv_s[h, ks, :] += dv
                else:
                    dv_s[h, ks, :] = dv
            delta = jnp.sum(ot * dot_[:, qs], axis=0, keepdims=True)
            o_s[h, qs, :] = ot.T
            dqt = None
            for kb in range(qb + 1):
                ks = slice(kb * ch, (kb + 1) * ch)
                dpt = mm(v_s[h, ks, :], do, NT)
                ds = (st[kb] * (dpt - delta)).astype(bf)
                o = mm(kt[:, ks], ds)
                dqt = o if dqt is None else dqt + o
                dk = mm(ds, q)
                if kb < qb:
                    dk_s[h, ks, :] += dk
                else:
                    dk_s[h, ks, :] = dk
            dq_s[h, qs, :] = dqt.T * 0.125
        return 0

    for hh in range(nh):
        head(hh, 0)

    for p in range(nch):
        rows = pl.ds(pl.multiple_of((p ^ head_at) * ch, ch), ch)
        parts = []
        for h in range(nh):
            parts += [dq_s[h, rows, :], dk_s[h, rows, :], dv_s[h, rows, :]]
        parts.append(jnp.zeros((ch, 64), f32))
        d = jnp.concatenate(parts, axis=1).astype(bf).astype(f32)
        d = rope(d, cs_s[0, rows, :], cs_s[1, rows, :], True)
        placed = pltpu.roll(d, HW * odd, 1).astype(bf)
        d = d.astype(bf)
        gb_ref[...] += jnp.sum(d.astype(f32), axis=0, keepdims=True)
        dn = mm(placed, w_ref[...], NT)
        n, _ = norm_parts(x_s[p].astype(f32))
        ln_ref[0:1, :] += jnp.sum(dn * n, axis=0, keepdims=True)
        ln_ref[1:2, :] += jnp.sum(dn, axis=0, keepdims=True)
        e = dn * gain
        if p < 2:
            e = e + me_ref[p, 0].astype(f32)
        (es_ref if p % 2 else e_ref)[p // 2, 0] = e.astype(bf)
        gw_s[0:real, :] += mm(d.T[0:real], nb_s[rows, :])
        ctx = jnp.concatenate([o_s[h, rows, :] for h in range(nh)], axis=1).astype(bf)
        (ctx_ref if p < 2 else ctxs_ref)[p % 2, 0] = ctx
        gw_s[real:, :] += mm(ctx.T, g_s[p])

    if last:
        @pl.when(pl.program_id(0) == pl.num_programs(0) - 1)
        def _():
            put_halves(gw_s, gw_s.shape[0] // 2, keep_ref, send_ref, own_ref[2], own_ref[3])
            v_ref[...] = jnp.zeros_like(v_ref)
            for u, ref in enumerate((gb0_ref, gb1_ref)):
                v_ref[pl.ds(own_ref[1] * 2 + u, 1), :] = ref[0:1, :]
            v_ref[pl.ds(4 + own_heads(own_ref), 1), 0:real] = gb_ref[:, 0:real]
            v_ref[8:9, :] = gb0_ref[1:2, :]
            v_ref[9:11, :] = ln_ref[0:2, :]
            v_ref[11:13, :] = ln2_ref[0:2, :]


def attention(own, r0, nr, last, xs, gs, w, w_out, vecs, cos, sin, start, me, before, held, sums, nz):
    rows_all, span, d = xs[0].shape
    row_len = start.shape[2]
    hd = w_out.shape[0] // 4
    nh = hd // HW
    real = nh * 3 * HW
    width = real + HW
    high = real + hd
    first = before is None
    spec = pl.BlockSpec
    at_row = lambda *s: spec((1,) + s, lambda i, o: (r0 + i, 0, 0))
    two = lambda *s: spec((2, 1) + s, lambda i, o: (0, r0 + i, 0, 0))
    whole = lambda *s: spec(s, lambda i, o: (0,) * len(s))
    shape = jax.ShapeDtypeStruct
    pieces = (nz, high // (2 * nz), d)
    outs = [shape((2, rows_all, span, hd), bf)] * 2 + [shape((2, rows_all, span, d), bf)] * 2
    ospecs = [two(span, hd)] * 2 + [two(span, d)] * 2
    sum_shapes = [(high, d), (1, width), (8, d)]
    if last:
        outs += [shape(pieces, bf)] * 2 + [shape((16, d), f32)]
        ospecs += [whole(*pieces)] * 2 + [whole(16, d)]
    else:
        outs += [shape(t, f32) for t in sum_shapes]
        ospecs += [whole(*t) for t in sum_shapes]
    heads = lambda dt: pltpu.VMEM((nh, row_len, HW), dt)
    scratch = [pltpu.VMEM((4, span, d), bf)] * 2 + [pltpu.VMEM((row_len, d), bf)] + [heads(bf)] * 4 + [heads(f32)] * 4 + [
        pltpu.VMEM((2, row_len, 2 * HW), f32), pltpu.VMEM((1, width), f32), pltpu.VMEM((d, width), bf)]
    window = lambda k: spec((d, 128), lambda i, o: (0, own_heads(o) * real // 128 + k))
    ins = [at_row(span, d)] * 8 + [window(k) for k in range(width // 128)] + [
        spec((hd, d), lambda i, o: (own_heads(o), 0)), whole(*vecs.shape), at_row(*cos.shape[1:]), at_row(*cos.shape[1:]),
        at_row(1, row_len), two(span, d)]
    args = [own, *xs, *gs, *[w] * (width // 128), w_out, vecs, cos, sin, start, me]
    alias = {}
    if not first:
        ins += [whole(*t) for t in sum_shapes]
        args += list(before)
        alias = {len(args) + k: k for k in range(4)}
        ins += [spec(memory_space=pl.ANY)] * 4
        args += list(held)
    if last:
        scratch += [pltpu.VMEM(t, f32) for t in sum_shapes]
        ins += [whole(8, d)] * 3
        args += list(sums)
    return pl.pallas_call(
        functools.partial(attn_body, first, last),
        out_shape=tuple(outs),
        grid_spec=pltpu.PrefetchScalarGridSpec(num_scalar_prefetch=1, grid=(nr,), in_specs=ins, out_specs=ospecs, scratch_shapes=scratch),
        input_output_aliases=alias,
        compiler_params=pltpu.CompilerParams(vmem_limit_bytes=60 * 2**20),
        cost_estimate=pl.CostEstimate(flops=nr * row_len * (8 * d * real + 6 * row_len * hd * 4), bytes_accessed=20 * 2**20, transcendentals=nr * nh * row_len * row_len // 2),
        name="attention%d" % r0,
    )(*args)


def own_heads(own):
    return own[1] * 2 + own[0]


def far_heads(own):
    return own[1] * 2 + 1 - own[0]


def project_body(own_ref, mine_ref, came_ref, wm_ref, wf_ref, mo_ref, keep_ref, send_ref):
    _, nr, span, _ = mine_ref.shape
    for r in range(nr):
        rows = slice(r * span, (r + 1) * span)
        for p, out_ref in enumerate((keep_ref, send_ref)):
            out_ref[rows, :] = (mm(mine_ref[p, r], wm_ref[...]) + mm(came_ref[p, r], wf_ref[...]) + mo_ref[p, rows, :].astype(f32)).astype(bf)


def project(own, mine, came, w_out, m_out):
    _, toks, d = m_out.shape
    hd = mine.shape[3]
    spec = pl.BlockSpec
    whole = lambda *s: spec(s, lambda i, o: (0,) * len(s))
    shape = jax.ShapeDtypeStruct
    return pl.pallas_call(
        project_body,
        out_shape=(shape((toks, d), bf), shape((toks, d), bf)),
        grid_spec=pltpu.PrefetchScalarGridSpec(
            num_scalar_prefetch=1, grid=(1,),
            in_specs=[whole(*mine.shape)] * 2 + [
                spec((hd, d), lambda i, o: (own_heads(o), 0)), spec((hd, d), lambda i, o: (far_heads(o), 0)), whole(2, toks, d)],
            out_specs=[whole(toks, d)] * 2,
        ),
        compiler_params=pltpu.CompilerParams(vmem_limit_bytes=60 * 2**20),
        name="project",
    )(own, mine, came, w_out, w_out, m_out)


from jax.sharding import PartitionSpec as P

HEADS = 12


def swap(x, axis, bit):
    n = lax.axis_size(axis)
    return lax.ppermute(x, axis, [(i, i ^ bit) for i in range(n)])


def add(a, b):
    return (a.astype(f32) + b.astype(f32)).astype(bf)


def tie(*groups):
    return lax.optimization_barrier(groups)


def hop(x, dp_bit, head_bit):
    nd, nh = lax.axis_size("dp"), lax.axis_size("head")
    return lax.ppermute(x, ("dp", "head"), [(i * nh + j, (i ^ dp_bit) * nh + (j ^ head_bit)) for i in range(nd) for j in range(nh)])


def cross(pieces, nz):
    return [swap(pieces[k], "dp", 2 * k) for k in range(1, nz)]


def gather_z(piece, nz):
    return [piece] + [swap(piece, "dp", 2 * k) for k in range(1, nz)]


def total(first, came):
    t = first.astype(f32)
    for c in came:
        t = t + c.astype(f32)
    return t.astype(bf)


def gather_vectors(vectors, d):
    def body(*refs):
        out_ref = refs[-1]
        out_ref[...] = jnp.zeros_like(out_ref)
        at = 0
        for ref in refs[:-1]:
            n = ref.shape[0]
            row = ref[...].astype(f32).reshape(1, n)
            for k in range(n // d):
                out_ref[at + k:at + k + 1, :] = row[:, k * d:(k + 1) * d]
            at += n // d

    vm = pl.BlockSpec(memory_space=pltpu.VMEM)
    return pl.pallas_call(
        body,
        out_shape=jax.ShapeDtypeStruct((VECS, d), f32),
        in_specs=[vm] * len(vectors),
        out_specs=vm,
        compiler_params=pltpu.CompilerParams(vmem_limit_bytes=60 * 2**20),
        name="vectors",
    )(*vectors)


def tables(lengths, row_len):
    pos = jnp.arange(row_len, dtype=jnp.int32)[None, :]
    first_end = lengths[:, 0:1]
    second_end = first_end + lengths[:, 1:2]
    start = jnp.where(pos < first_end, 0, jnp.where(pos < second_end, first_end, second_end))
    half = ROT // 2
    freq = 1.0 / 10000.0 ** (jnp.arange(half, dtype=f32) * 2.0 / ROT)
    angle = (pos - start)[:, None, :].astype(f32) * freq[None, :, None]

    return jnp.cos(angle), jnp.sin(angle), start[:, None, :]


def fill_body(nu, pieces_ref, wi_ref, wd_ref):
    d = pieces_ref.shape[-1]
    for c in range(2):
        for u in range(nu):
            b = c * nu + u
            wi_ref[:, b * d:(b + 1) * d] = pieces_ref[0, c, u].astype(f32)
            wd_ref[b, 0] = pieces_ref[1, c, u].astype(f32)


def fill_mlp(pieces):
    nd, nh, nu, rows, d = pieces.shape
    wi, wd = pl.pallas_call(
        functools.partial(fill_body, nu),
        grid=(nd,),
        out_shape=(jax.ShapeDtypeStruct((nd * rows, 2 * nu * d), f32), jax.ShapeDtypeStruct((2 * nu, nd, rows, d), f32)),
        in_specs=[pl.BlockSpec((None, 2, 2, nu, rows, d), lambda i: (i, 0, 0, 0, 0, 0))],
        out_specs=(pl.BlockSpec((rows, 2 * nu * d), lambda i: (i, 0)), pl.BlockSpec((2 * nu, 1, rows, d), lambda i: (0, i, 0, 0))),
        compiler_params=pltpu.CompilerParams(vmem_limit_bytes=60 * 2**20),
        name="fill_mlp",
    )(pieces.reshape(nd, 2, 2, nu, rows, d))
    return wi, wd.reshape(2 * nu * nd * rows, d)


def fill_attn(own, arrays, real):
    nz, rows, d = arrays[0].shape
    high = 2 * nz * rows
    lanes = 256
    parts = [(0, 0, 0), (1, 0, 0), (0, 1, 0), (1, 1, 0), (1, 1, nz // 2)]

    def body(own_ref, *refs):
        wq_ref, wo_ref, s = refs[10:]
        x, c, y, z = own_ref[0], own_ref[1], own_ref[2], own_ref[3]
        for k in range(10):
            jx, jy, lo = parts[k % 5]
            block = (c ^ (k // 5)) * 2 + (x ^ jx)
            for t in range(refs[k].shape[0]):
                at = pl.multiple_of(((y ^ jy) * nz + (z ^ (lo + t))) * rows, 8)
                s[block, pl.ds(at, rows), :] = refs[k][t].astype(f32)
        for b in range(4):
            wq_ref[:, b * real:(b + 1) * real] = s[b, 0:real].T
            wo_ref[b * (high - real):(b + 1) * (high - real), :] = s[b, real:]

    return pl.pallas_call(
        body,
        out_shape=(jax.ShapeDtypeStruct((d, 4 * real), f32), jax.ShapeDtypeStruct((d, d), f32)),
        grid_spec=pltpu.PrefetchScalarGridSpec(
            num_scalar_prefetch=1, grid=(d // lanes,),
            in_specs=[pl.BlockSpec((a.shape[0], rows, lanes), lambda i, o: (0, 0, i)) for a in arrays],
            out_specs=(pl.BlockSpec((lanes, 4 * real), lambda i, o: (i, 0)), pl.BlockSpec((d, lanes), lambda i, o: (0, i))),
            scratch_shapes=[pltpu.VMEM((4, high, lanes), f32)],
        ),
        compiler_params=pltpu.CompilerParams(vmem_limit_bytes=60 * 2**20),
        name="fill_attn",
    )(own, *arrays)


def on_device(tokens, lengths, w_qkv, b_qkv, w_out, b_out, w_in, b_in, w_down, b_down,
              norm1_gain, norm1_bias, norm2_gain, norm2_bias, cotangent):
    rows, span, d = tokens.shape
    ff = w_in.shape[1]
    head = lax.axis_index("head")
    dp = lax.axis_index("dp")
    x, c = head // 2, head % 2
    y, z = dp % 2, dp // 2
    nz = lax.axis_size("dp") // 2
    own = jnp.stack([x, c, y, z]).astype(jnp.int32)
    row_len = 4 * span
    hd = HEADS // 4 * HW
    flat = lambda a: a.reshape(-1, d)

    gpar = swap(cotangent, "head", 1)
    par = swap(tokens, "head", 1)
    far = swap(tokens, "head", 2)
    gfar = swap(cotangent, "head", 2)
    go, gp = flat(cotangent), flat(gpar)
    xo, xp = flat(tokens), flat(par)
    small = [b_in, b_qkv, b_out, norm1_gain, norm1_bias, norm2_gain, norm2_bias, b_down]
    vecs = gather_vectors(small, d)

    o0, h0, *u0, gb0 = mlp(own, 0, xo, xp, go, gp, w_in, w_down, vecs, nz)
    far, o0, u0, lengths = tie(far, o0, u0, lengths)

    u0r = [swap(u0[1], "dp", 1), swap(u0[3], "dp", 1)]
    farpar = swap(far, "head", 1)
    m_out, m_e, *u1, gb1, ln2 = mlp(own, 1, xo, xp, go, gp, w_in, w_down, vecs, nz, (o0, h0))
    farpar, gfar, u0r, m_out, m_e, u1, lengths = tie(farpar, gfar, u0r, m_out, m_e, u1, lengths)

    gfarpar = swap(gfar, "head", 1)
    u1r = [swap(u1[1], "dp", 1), swap(u1[2], "head", 2), hop(u1[3], 1, 2)]
    u0s, u0 = add(u0[2], u0r[1]), add(u0[0], u0r[0])
    u0r = swap(u0s, "head", 2)
    cos, sin, start = tables(lengths, row_len)
    gfarpar, cos, sin, start = tie(gfarpar, cos, sin, start)
    xs = (tokens, par, far, farpar)
    gs = (cotangent, gpar, gfar, gfarpar)
    me = m_e.reshape(2, rows, span, d)

    def attend(r, w, state, held):
        return attention(own, r, 1, r == rows - 1, xs, gs, w, w_out, vecs, cos, sin, start, me, state, held, (gb0, gb1, ln2), nz)

    *held, gw, gb, ln = attend(0, w_qkv, None, None)
    u0r, u1r, held, gw, gb, ln = tie(u0r, u1r, held, gw, gb, ln)

    u = jnp.stack([add(u0, u0r), total(u1[0], u1r)], axis=1)
    uz = cross(u, nz)
    *held, gw, gb, ln = attend(1, w_qkv, (gw, gb, ln), held)
    uz, held, gw, gb, ln = tie(uz, held, gw, gb, ln)

    whole = lax.all_gather(total(u[0], uz), ("dp", "head"))
    ctx, ctxs, e, es, qk, qs, v = attend(2, w_qkv, (gw, gb, ln), held)
    ctx, ctxs, e, es, qk, qs, v = tie(ctx, ctxs, e, es, qk, qs, v)

    qr = swap(qs, "dp", 1)
    ctxr = swap(ctxs, "head", 2)
    er = swap(es, "head", 1)
    v1 = swap(v, "dp", 2)
    qr, er, v1 = tie(qr, er, v1)

    q = add(qk, qr)
    qr = cross(q, nz)
    ex = swap(add(e[1], er[1]), "head", 2)
    v = v + v1
    v1 = swap(v, "head", 1)
    qr, v1, ctxr = tie(qr, v1, ctxr)

    q = gather_z(total(q[0], qr), nz)
    v = v + v1
    v1 = swap(v, "head", 2)
    keep, send = project(own, ctx, ctxr, w_out, m_out.reshape(2, rows * span, d))
    q, v1, keep, send, ex = tie(q, v1, keep, send, ex)

    zq = jnp.stack(q)
    xq = swap(zq, "head", 2)
    yq = swap(zq, "dp", 1)
    cz = swap(zq, "head", 1)
    outr = swap(send, "head", 1)
    v = v + v1
    bit = 4
    while bit < 2 * nz:
        v = v + swap(v, "dp", bit)
        bit *= 2
    es = e[0].astype(f32) + er[0].astype(f32) + ex.astype(f32)
    n, rho = norm_parts(tokens.astype(f32))
    dx = rho * (es - jnp.mean(es, -1, keepdims=True) - n * jnp.mean(es * n, -1, keepdims=True))
    grad_tokens = (cotangent.astype(f32) + dx).astype(bf)
    grad_w_in, grad_w_down = fill_mlp(whole.reshape((2 * nz, 4) + whole.shape[1:]))
    xq, yq, cz, v, outr, grad_tokens, grad_w_in, grad_w_down = tie(xq, yq, cz, v, outr, grad_tokens, grad_w_in, grad_w_down)

    d0 = swap(yq[:nz // 2], "head", 2)
    d1 = swap(xq[nz // 2:], "dp", 1)
    cx, cy = swap(xq, "head", 1), swap(yq, "head", 1)
    v = v + swap(v, "dp", 1)
    shape = (rows, span, d)
    output = (tokens.astype(f32) + keep.astype(f32).reshape(shape) + outr.astype(f32).reshape(shape)
              + (b_out.astype(f32) + b_down.astype(f32))).astype(bf)
    d0, d1, cx, cy, v, output = tie(d0, d1, cx, cy, v, output)

    c0, c1 = swap(d0, "head", 1), swap(d1, "head", 1)
    parts = (v[4:8, :3 * hd].reshape(-1), v[0:4].reshape(-1), v[8], v[9], v[10], v[11], v[12])
    c0, c1, parts = tie(c0, c1, parts)
    grad_w_qkv, grad_w_out = fill_attn(own, (zq, xq, yq, d0, d1, cz, cx, cy, c0, c1), 3 * hd)

    return (output, grad_tokens, grad_w_qkv, parts[0], grad_w_out, parts[2], grad_w_in, parts[1],
            grad_w_down, parts[2], *parts[3:])


def solution(mesh):
    split = P("dp", "head", None)
    return jax.shard_map(
        on_device, mesh=mesh,
        in_specs=(split, P("dp", None)) + (P(),) * 12 + (split,),
        out_specs=(split, split) + (P(),) * 12,
        check_vma=False,
    )
```

```python
import math, functools
import jax
import jax.numpy as jnp
from jax import lax
from jax.experimental import pallas as pl
from jax.experimental.pallas import tpu as pltpu

bf = jnp.bfloat16
f32 = jnp.float32
NN = (((1,), (0,)), ((), ()))
NT = (((1,), (1,)), ((), ()))
TN = (((0,), (0,)), ((), ()))


def mm(a, b, dims=NN):
    return lax.dot_general(a, b, dims, preferred_element_type=f32)


def norm_parts(x):
    center = x - jnp.mean(x, axis=-1, keepdims=True)
    rho = lax.rsqrt(jnp.mean(center * center, axis=-1, keepdims=True) + 1e-5)
    return center * rho, rho


def normal_cdf(x):
    bell = jnp.exp(-0.5 * x * x)
    t = 1.0 / (1.0 + (0.3275911 * math.sqrt(0.5)) * jnp.abs(x))
    poly = t * (0.127414796 + t * (-0.142248368 + t * (0.7107068705 + t * (-0.7265760135 + t * 0.5307027145))))
    tail = poly * bell
    return jnp.where(x >= 0, 1.0 - tail, tail), bell


def put_quarters(acc, kind, refs, x, y, z):
    nz, rows = refs[0].shape[0], refs[0].shape[1]
    for hy in range(2):
        for at, ref in enumerate(refs):
            jx, jy = at // 2, at % 2

            @pl.when(((x ^ kind) == jx) & ((y ^ hy) == jy))
            def _():
                for hz in range(nz):
                    row = (hz * 2 + hy) * rows
                    ref[hz ^ z] = acc[row:row + rows, :].astype(bf)


def put_halves(acc, half, keep_ref, send_ref, y, z):
    nz, rows = keep_ref.shape[0], keep_ref.shape[1]
    for hy in range(2):
        for ref, stays in ((keep_ref, True), (send_ref, False)):
            @pl.when((y == hy) == stays)
            def _():
                for hz in range(nz):
                    at = hy * half + hz * rows
                    ref[hz ^ z] = acc[at:at + rows, :].astype(bf)


B_IN, B_QKV, B_LAST, GAIN1, BIAS1, GAIN2, BIAS2, VECS = 0, 4, 7, 8, 9, 10, 11, 16


def vector(vec_ref, k, d, count=1):
    return jnp.concatenate([vec_ref[pl.ds(k + i, 1), :] for i in range(count)], axis=1)


def mlp_body(first, own_ref, xo_ref, xp_ref, go_ref, gp_ref, wi_ref, wd_ref, vec_ref, *rest):
    if first:
        out_ref, dh_ref, g0_ref, g1_ref, g2_ref, g3_ref, gbi_ref, *rest = rest
    else:
        outp_ref, dhp_ref, out_ref, e_ref, g0_ref, g1_ref, g2_ref, g3_ref, gbi_ref, ln_ref, n_s, *rest = rest
    h_s, ht_s, g_s, gwi_s, gwd_s = rest
    i, ni = pl.program_id(0), pl.num_programs(0)
    d = xo_ref.shape[1]
    gain = vector(vec_ref, GAIN2, d)

    def start(x_ref, g_ref):
        n, _ = norm_parts(x_ref[...].astype(f32))
        h = (n * gain + vector(vec_ref, BIAS2, d)).astype(bf)
        if not first:
            n_s[...] = n
        h_s[...] = h
        ht_s[...] = h.T
        g_s[...] = g_ref[...]

    @pl.when(i == 0)
    def _():
        start(xo_ref, go_ref)

    @pl.when(i == 1)
    def _():
        start(xp_ref, gp_ref)

    unit = 0 if first else 1
    pre = mm(h_s[...], wi_ref[...]) + vector(vec_ref, B_IN + own_ref[1] * 2 + unit, d)
    d_act = mm(g_s[...], wd_ref[...], NT)
    cdf, bell = normal_cdf(pre)
    act = (pre * cdf).astype(bf)
    slope = cdf + pre * bell * (1.0 / math.sqrt(2.0 * math.pi))
    d_pre = (d_act * slope).astype(bf)
    out = mm(act, wd_ref[...])
    dh = mm(d_pre, wi_ref[...], NT)
    gwi = mm(ht_s[...], d_pre)
    gwd = mm(act.T, g_s[...])
    gbi = jnp.sum(d_pre.astype(f32), axis=0, keepdims=True)

    @pl.when(i == 0)
    def _():
        gwi_s[...] = gwi
        gwd_s[...] = gwd
        gbi_ref[0:1, :] = gbi
        gbi_ref[1:2, :] = jnp.sum(g_s[...].astype(f32), axis=0, keepdims=True)

    @pl.when(i == ni - 1)
    def _():
        gwi_s[...] += gwi
        gwd_s[...] += gwd
        gbi_ref[0:1, :] += gbi
        x, y, z = own_ref[0], own_ref[2], own_ref[3]
        gw = [g0_ref, g1_ref, g2_ref, g3_ref]
        put_quarters(gwi_s, 0, gw, x, y, z)
        put_quarters(gwd_s, 1, gw, x, y, z)

    if first:
        out_ref[...] = out.astype(bf)
        dh_ref[...] = dh.astype(bf)
    else:
        @pl.when(i == 0)
        def _():
            ln_ref[...] = jnp.zeros_like(ln_ref)

        dh = dh + dhp_ref[...].astype(f32)
        out_ref[...] = (out + outp_ref[...].astype(f32)).astype(bf)
        e_ref[...] = (dh * gain).astype(bf)
        ln_ref[0:1, :] += jnp.sum(dh * n_s[...], axis=0, keepdims=True)
        ln_ref[1:2, :] += jnp.sum(dh, axis=0, keepdims=True)


def mlp(own, unit, xo, xp, go, gp, w_in, w_down, vecs, nz, before=None):
    toks, d = xo.shape
    first = before is None
    rows = d // (2 * nz)
    spec = pl.BlockSpec
    once = lambda *s: spec(s, lambda i, o: (0,) * len(s), pipeline_mode=pl.Buffered(1))
    tile = spec((toks, d), lambda i, o: (i, 0))
    part = lambda o: o[1] * 2 + unit
    shape = jax.ShapeDtypeStruct
    vm = pltpu.VMEM
    ins = [once(toks, d)] * 4 + [spec((d, d), lambda i, o: (0, part(o)), pipeline_mode=pl.Buffered(1)),
                                 spec((d, d), lambda i, o: (part(o), 0), pipeline_mode=pl.Buffered(1)), once(*vecs.shape)]
    args = [own, xo, xp, go, gp, w_in, w_down, vecs]
    outs = [shape((2 * toks, d), bf), shape((2 * toks, d), bf)] + [shape((nz, rows, d), bf)] * 4 + [shape((8, d), f32)]
    ospecs = [tile, tile] + [once(nz, rows, d)] * 4 + [once(8, d)]
    scratch = [vm((toks, d), bf)] * 3 + [vm((d, d), f32)] * 2
    if not first:
        ins += [tile, tile]
        args += list(before)
        outs.append(shape((8, d), f32))
        ospecs.append(once(8, d))
        scratch = [vm((toks, d), f32)] + scratch
    return pl.pallas_call(
        functools.partial(mlp_body, first),
        out_shape=tuple(outs),
        grid_spec=pltpu.PrefetchScalarGridSpec(num_scalar_prefetch=1, grid=(2,), in_specs=ins, out_specs=ospecs, scratch_shapes=scratch),
        compiler_params=pltpu.CompilerParams(vmem_limit_bytes=60 * 2**20),
        cost_estimate=pl.CostEstimate(flops=24 * toks * d * d, bytes_accessed=20 * 2**20, transcendentals=2 * toks * d),
        name="mlp%d" % unit,
    )(*args)


HW = 64
ROT = 16


def rope(u, cos, sin, back):
    t, width = u.shape
    lane = lax.broadcasted_iota(jnp.int32, (t, 128), 1)
    inner = lane % HW
    low = inner < ROT // 2
    outs = []
    for b in range(width // 128):
        v = u[:, b * 128:(b + 1) * 128]
        lo_rot, hi_rot = (2 * b) % 3 != 2, (2 * b + 1) % 3 != 2
        if (2 * b + 1) * HW >= 9 * HW:
            hi_rot = False
        if not (lo_rot or hi_rot):
            outs.append(v)
            continue
        turned = inner < ROT
        if not hi_rot:
            turned = turned & (lane < HW)
        if not lo_rot:
            turned = turned & (lane >= HW)
        up = pltpu.roll(v, 128 - ROT // 2, 1)
        down = pltpu.roll(v, ROT // 2, 1)
        if back:
            swapped = jnp.where(low, up, -down)
        else:
            swapped = jnp.where(low, -up, down)
        outs.append(jnp.where(turned, v * cos + swapped * sin, v))
    return jnp.concatenate(outs, axis=1)


def attn_body(first, last, own_ref, xo_ref, xp_ref, xf_ref, xfp_ref, go_ref, gp_ref, gf_ref, gfp_ref, w0_ref, w1_ref, w2_ref, w3_ref, w4_ref, wo_ref, vec_ref,
              cos_ref, sin_ref, start_ref, me_ref, *rest):
    if not first:
        gwp_ref, gbp_ref, lnp_ref, *rest = rest
        rest = rest[4:]
    if last:
        gb0_ref, gb1_ref, ln2_ref, *rest = rest
    ctx_ref, ctxs_ref, e_ref, es_ref, *rest = rest
    if last:
        keep_ref, send_ref, v_ref, *scratch = rest
        gw_s, gb_ref, ln_ref = scratch[-3:]
    else:
        gw_s, gb_ref, ln_ref, *scratch = rest
    x_s, g_s, nb_s, q_s, k_s, v_s, do_s, o_s, dq_s, dk_s, dv_s, cs_s, b_ref, w_ref = scratch[:14]
    head_at = own_ref[0] * 2 + own_ref[1]
    ch = xo_ref.shape[1]
    row_len = start_ref.shape[2]
    nh = q_s.shape[0]
    nch = row_len // ch
    real = nh * 3 * HW
    d_model = x_s.shape[2]
    gain = vector(vec_ref, GAIN1, d_model)
    bias = vector(vec_ref, BIAS1, d_model)

    @pl.when(pl.program_id(0) == 0)
    def _():
        block = own_ref[1] * 2 + own_ref[0]
        b_ref[...] = jnp.zeros_like(b_ref)
        columns = vector(vec_ref, B_QKV, d_model, 3)
        for b in range(4):
            @pl.when(block == b)
            def _():
                b_ref[:, 0:real] = columns[:, b * real:(b + 1) * real]
        for k, ref in enumerate((w0_ref, w1_ref, w2_ref, w3_ref, w4_ref)):
            w_ref[:, k * 128:(k + 1) * 128] = ref[...]
        if first:
            gw_s[...] = jnp.zeros_like(gw_s)
            gb_ref[...] = jnp.zeros_like(gb_ref)
            ln_ref[...] = jnp.zeros_like(ln_ref)
        else:
            gw_s[...] = gwp_ref[...]
            gb_ref[...] = gbp_ref[...]
            ln_ref[...] = lnp_ref[...]

    width = w_ref.shape[1]
    odd = own_ref[0]
    back_by = (width - HW) * odd
    for t, (ref, rest_value) in enumerate(((cos_ref, 1.0), (sin_ref, 0.0))):
        one = ref[0]
        still = jnp.full((HW - ROT, row_len), rest_value, f32)
        cs_s[t] = jnp.concatenate([one, one, still, one, one, still], axis=0).T
    for p, (ref, ref2) in enumerate(((xo_ref, go_ref), (xp_ref, gp_ref), (xf_ref, gf_ref), (xfp_ref, gfp_ref))):
        x_s[p] = ref[0]
        g_s[p] = ref2[0]

    def project(p, _):
        ci = p ^ head_at
        rows = pl.ds(pl.multiple_of(ci * ch, ch), ch)
        n, _ = norm_parts(x_s[p].astype(f32))
        normed = (n * gain + bias).astype(bf)
        nb_s[rows, :] = normed
        lin = pltpu.roll(mm(normed, w_ref[...]), back_by, 1) + b_ref[...]
        lin = rope(lin, cs_s[0, rows, :], cs_s[1, rows, :], False)
        for h in range(nh):
            q_s[h, rows, :] = (lin[:, h * 192:h * 192 + 64].astype(bf) * bf(0.125))
            k_s[h, rows, :] = lin[:, h * 192 + 64:h * 192 + 128].astype(bf)
            v_s[h, rows, :] = lin[:, h * 192 + 128:h * 192 + 192].astype(bf)
        d_ctx = mm(g_s[p], wo_ref[...], NT).astype(bf)
        for h in range(nh):
            do_s[h, rows, :] = d_ctx[:, h * HW:(h + 1) * HW]
        return 0

    for p in range(nch):
        project(p, 0)
    def head(h, _):
        kt = k_s[h].T
        vt = v_s[h].T
        dot_ = do_s[h].astype(f32).T
        for qb in range(nch):
            k0, kn = qb * ch, (qb + 1) * ch
            qs = slice(k0, kn)
            q = q_s[h, qs, :]
            do = do_s[h, qs, :]
            first = start_ref[0, :, qs]
            kpos = lax.broadcasted_iota(jnp.int32, (ch, ch), 0)
            qpos = lax.broadcasted_iota(jnp.int32, (ch, ch), 1)
            st = []
            top = None
            for kb in range(qb + 1):
                s = mm(k_s[h, kb * ch:(kb + 1) * ch, :], q, NT)
                keep = kpos >= first - kb * ch
                if kb == qb:
                    keep = keep & (kpos <= qpos)
                s = jnp.where(keep, s, -1e9)
                m = jnp.max(s, axis=0, keepdims=True)
                top = m if top is None else jnp.maximum(top, m)
                st.append(s)
            size = None
            for kb in range(qb + 1):
                st[kb] = jnp.exp(st[kb] - top)
                m = jnp.sum(st[kb], axis=0, keepdims=True)
                size = m if size is None else size + m
            inv = 1.0 / size
            ot = None
            for kb in range(qb + 1):
                ks = slice(kb * ch, (kb + 1) * ch)
                st[kb] = st[kb] * inv
                pb = st[kb].astype(bf)
                o = mm(vt[:, ks], pb)
                ot = o if ot is None else ot + o
                dv = mm(pb, do)
                if kb < qb:
                    dv_s[h, ks, :] += dv
                else:
                    dv_s[h, ks, :] = dv
            delta = jnp.sum(ot * dot_[:, qs], axis=0, keepdims=True)
            o_s[h * HW:(h + 1) * HW, qs] = ot.astype(bf)
            dqt = None
            for kb in range(qb + 1):
                ks = slice(kb * ch, (kb + 1) * ch)
                dpt = mm(v_s[h, ks, :], do, NT)
                ds = (st[kb] * (dpt - delta)).astype(bf)
                o = mm(kt[:, ks], ds)
                dqt = o if dqt is None else dqt + o
                dk = mm(ds, q)
                if kb < qb:
                    dk_s[h, ks, :] += dk
                else:
                    dk_s[h, ks, :] = dk
            dq_s[h, qs, :] = dqt.T * 0.125
        return 0

    for hh in range(nh):
        head(hh, 0)

    for p in range(nch):
        rows = pl.ds(pl.multiple_of((p ^ head_at) * ch, ch), ch)
        parts = []
        for h in range(nh):
            parts += [dq_s[h, rows, :], dk_s[h, rows, :], dv_s[h, rows, :]]
        parts.append(jnp.zeros((ch, 64), f32))
        d = jnp.concatenate(parts, axis=1).astype(bf).astype(f32)
        d = rope(d, cs_s[0, rows, :], cs_s[1, rows, :], True)
        placed = pltpu.roll(d, HW * odd, 1).astype(bf)
        d = d.astype(bf)
        gb_ref[...] += jnp.sum(d.astype(f32), axis=0, keepdims=True)
        dn = mm(placed, w_ref[...], NT)
        n, _ = norm_parts(x_s[p].astype(f32))
        ln_ref[0:1, :] += jnp.sum(dn * n, axis=0, keepdims=True)
        ln_ref[1:2, :] += jnp.sum(dn, axis=0, keepdims=True)
        e = dn * gain
        if p < 2:
            e = e + me_ref[p, 0].astype(f32)
        (es_ref if p % 2 else e_ref)[p // 2, 0] = e.astype(bf)
        gw_s[0:real, :] += mm(d.T[0:real], nb_s[rows, :])
        ctx = o_s[:, rows]
        (ctx_ref if p < 2 else ctxs_ref)[p % 2, 0] = ctx
        gw_s[real:, :] += mm(ctx, g_s[p])

    if last:
        @pl.when(pl.program_id(0) == pl.num_programs(0) - 1)
        def _():
            put_halves(gw_s, gw_s.shape[0] // 2, keep_ref, send_ref, own_ref[2], own_ref[3])
            v_ref[...] = jnp.zeros_like(v_ref)
            for u, ref in enumerate((gb0_ref, gb1_ref)):
                v_ref[pl.ds(own_ref[1] * 2 + u, 1), :] = ref[0:1, :]
            v_ref[pl.ds(4 + own_heads(own_ref), 1), 0:real] = gb_ref[:, 0:real]
            v_ref[8:9, :] = gb0_ref[1:2, :]
            v_ref[9:11, :] = ln_ref[0:2, :]
            v_ref[11:13, :] = ln2_ref[0:2, :]


def attention(own, r0, nr, last, xs, gs, w, w_out, vecs, cos, sin, start, me, before, held, sums, nz):
    rows_all, span, d = xs[0].shape
    row_len = start.shape[2]
    hd = w_out.shape[0] // 4
    nh = hd // HW
    real = nh * 3 * HW
    width = real + HW
    high = real + hd
    first = before is None
    spec = pl.BlockSpec
    at_row = lambda *s: spec((1,) + s, lambda i, o: (r0 + i, 0, 0))
    two = lambda *s: spec((2, 1) + s, lambda i, o: (0, r0 + i, 0, 0))
    whole = lambda *s: spec(s, lambda i, o: (0,) * len(s))
    shape = jax.ShapeDtypeStruct
    pieces = (nz, high // (2 * nz), d)
    outs = [shape((2, rows_all, hd, span), bf)] * 2 + [shape((2, rows_all, span, d), bf)] * 2
    ospecs = [two(hd, span)] * 2 + [two(span, d)] * 2
    sum_shapes = [(high, d), (1, width), (8, d)]
    if last:
        outs += [shape(pieces, bf)] * 2 + [shape((16, d), f32)]
        ospecs += [whole(*pieces)] * 2 + [whole(16, d)]
    else:
        outs += [shape(t, f32) for t in sum_shapes]
        ospecs += [whole(*t) for t in sum_shapes]
    heads = lambda dt: pltpu.VMEM((nh, row_len, HW), dt)
    scratch = [pltpu.VMEM((4, span, d), bf)] * 2 + [pltpu.VMEM((row_len, d), bf)] + [heads(bf)] * 4 + [pltpu.VMEM((hd, row_len), bf)] + [heads(f32)] * 3 + [
        pltpu.VMEM((2, row_len, 2 * HW), f32), pltpu.VMEM((1, width), f32), pltpu.VMEM((d, width), bf)]
    window = lambda k: spec((d, 128), lambda i, o: (0, own_heads(o) * real // 128 + k))
    ins = [at_row(span, d)] * 8 + [window(k) for k in range(width // 128)] + [
        spec((hd, d), lambda i, o: (own_heads(o), 0)), whole(*vecs.shape), at_row(*cos.shape[1:]), at_row(*cos.shape[1:]),
        at_row(1, row_len), two(span, d)]
    args = [own, *xs, *gs, *[w] * (width // 128), w_out, vecs, cos, sin, start, me]
    alias = {}
    if not first:
        ins += [whole(*t) for t in sum_shapes]
        args += list(before)
        alias = {len(args) + k: k for k in range(4)}
        ins += [spec(memory_space=pl.ANY)] * 4
        args += list(held)
    if last:
        scratch += [pltpu.VMEM(t, f32) for t in sum_shapes]
        ins += [whole(8, d)] * 3
        args += list(sums)
    return pl.pallas_call(
        functools.partial(attn_body, first, last),
        out_shape=tuple(outs),
        grid_spec=pltpu.PrefetchScalarGridSpec(num_scalar_prefetch=1, grid=(nr,), in_specs=ins, out_specs=ospecs, scratch_shapes=scratch),
        input_output_aliases=alias,
        compiler_params=pltpu.CompilerParams(vmem_limit_bytes=60 * 2**20),
        cost_estimate=pl.CostEstimate(flops=nr * row_len * (8 * d * real + 6 * row_len * hd * 4), bytes_accessed=20 * 2**20, transcendentals=nr * nh * row_len * row_len // 2),
        name="attention%d" % r0,
    )(*args)


def own_heads(own):
    return own[1] * 2 + own[0]


def far_heads(own):
    return own[1] * 2 + 1 - own[0]


def project_body(own_ref, mine_ref, came_ref, wm_ref, wf_ref, mo_ref, keep_ref, send_ref):
    _, nr, _, span = mine_ref.shape
    for r in range(nr):
        rows = slice(r * span, (r + 1) * span)
        for p, out_ref in enumerate((keep_ref, send_ref)):
            out_ref[rows, :] = (mm(mine_ref[p, r], wm_ref[...], TN) + mm(came_ref[p, r], wf_ref[...], TN) + mo_ref[p, rows, :].astype(f32)).astype(bf)


def project(own, mine, came, w_out, m_out):
    _, toks, d = m_out.shape
    hd = mine.shape[2]
    spec = pl.BlockSpec
    whole = lambda *s: spec(s, lambda i, o: (0,) * len(s))
    shape = jax.ShapeDtypeStruct
    return pl.pallas_call(
        project_body,
        out_shape=(shape((toks, d), bf), shape((toks, d), bf)),
        grid_spec=pltpu.PrefetchScalarGridSpec(
            num_scalar_prefetch=1, grid=(1,),
            in_specs=[whole(*mine.shape)] * 2 + [
                spec((hd, d), lambda i, o: (own_heads(o), 0)), spec((hd, d), lambda i, o: (far_heads(o), 0)), whole(2, toks, d)],
            out_specs=[whole(toks, d)] * 2,
        ),
        compiler_params=pltpu.CompilerParams(vmem_limit_bytes=60 * 2**20),
        name="project",
    )(own, mine, came, w_out, w_out, m_out)


from jax.sharding import PartitionSpec as P

HEADS = 12


def swap(x, axis, bit):
    n = lax.axis_size(axis)
    return lax.ppermute(x, axis, [(i, i ^ bit) for i in range(n)])


def add(a, b):
    return (a.astype(f32) + b.astype(f32)).astype(bf)


def tie(*groups):
    return lax.optimization_barrier(groups)


def hop(x, dp_bit, head_bit):
    nd, nh = lax.axis_size("dp"), lax.axis_size("head")
    return lax.ppermute(x, ("dp", "head"), [(i * nh + j, (i ^ dp_bit) * nh + (j ^ head_bit)) for i in range(nd) for j in range(nh)])


def cross(pieces, nz):
    return [swap(pieces[k], "dp", 2 * k) for k in range(1, nz)]


def gather_z(piece, nz):
    return [piece] + [swap(piece, "dp", 2 * k) for k in range(1, nz)]


def total(first, came):
    t = first.astype(f32)
    for c in came:
        t = t + c.astype(f32)
    return t.astype(bf)


def gather_vectors(vectors, d):
    def body(*refs):
        out_ref = refs[-1]
        out_ref[...] = jnp.zeros_like(out_ref)
        at = 0
        for ref in refs[:-1]:
            n = ref.shape[0]
            row = ref[...].astype(f32).reshape(1, n)
            for k in range(n // d):
                out_ref[at + k:at + k + 1, :] = row[:, k * d:(k + 1) * d]
            at += n // d

    vm = pl.BlockSpec(memory_space=pltpu.VMEM)
    return pl.pallas_call(
        body,
        out_shape=jax.ShapeDtypeStruct((VECS, d), f32),
        in_specs=[vm] * len(vectors),
        out_specs=vm,
        compiler_params=pltpu.CompilerParams(vmem_limit_bytes=60 * 2**20),
        name="vectors",
    )(*vectors)


def tables(lengths, row_len):
    pos = jnp.arange(row_len, dtype=jnp.int32)[None, :]
    first_end = lengths[:, 0:1]
    second_end = first_end + lengths[:, 1:2]
    start = jnp.where(pos < first_end, 0, jnp.where(pos < second_end, first_end, second_end))
    half = ROT // 2
    freq = 1.0 / 10000.0 ** (jnp.arange(half, dtype=f32) * 2.0 / ROT)
    angle = (pos - start)[:, None, :].astype(f32) * freq[None, :, None]

    return jnp.cos(angle), jnp.sin(angle), start[:, None, :]


def fill_body(nu, pieces_ref, wi_ref, wd_ref):
    d = pieces_ref.shape[-1]
    for c in range(2):
        for u in range(nu):
            b = c * nu + u
            wi_ref[:, b * d:(b + 1) * d] = pieces_ref[0, c, u].astype(f32)
            wd_ref[b, 0] = pieces_ref[1, c, u].astype(f32)


def fill_mlp(pieces):
    nd, nh, nu, rows, d = pieces.shape
    wi, wd = pl.pallas_call(
        functools.partial(fill_body, nu),
        grid=(nd,),
        out_shape=(jax.ShapeDtypeStruct((nd * rows, 2 * nu * d), f32), jax.ShapeDtypeStruct((2 * nu, nd, rows, d), f32)),
        in_specs=[pl.BlockSpec((None, 2, 2, nu, rows, d), lambda i: (i, 0, 0, 0, 0, 0))],
        out_specs=(pl.BlockSpec((rows, 2 * nu * d), lambda i: (i, 0)), pl.BlockSpec((2 * nu, 1, rows, d), lambda i: (0, i, 0, 0))),
        compiler_params=pltpu.CompilerParams(vmem_limit_bytes=60 * 2**20),
        name="fill_mlp",
    )(pieces.reshape(nd, 2, 2, nu, rows, d))
    return wi, wd.reshape(2 * nu * nd * rows, d)


def fill_attn(own, arrays, real):
    nz, rows, d = arrays[0].shape
    high = 2 * nz * rows
    lanes = 256
    parts = [(0, 0, 0), (1, 0, 0), (0, 1, 0), (1, 1, 0), (1, 1, nz // 2)]

    def body(own_ref, *refs):
        wq_ref, wo_ref, s = refs[10:]
        x, c, y, z = own_ref[0], own_ref[1], own_ref[2], own_ref[3]
        for k in range(10):
            jx, jy, lo = parts[k % 5]
            block = (c ^ (k // 5)) * 2 + (x ^ jx)
            for t in range(refs[k].shape[0]):
                at = pl.multiple_of(((y ^ jy) * nz + (z ^ (lo + t))) * rows, 8)
                s[block, pl.ds(at, rows), :] = refs[k][t].astype(f32)
        for b in range(4):
            wq_ref[:, b * real:(b + 1) * real] = s[b, 0:real].T
            wo_ref[b * (high - real):(b + 1) * (high - real), :] = s[b, real:]

    return pl.pallas_call(
        body,
        out_shape=(jax.ShapeDtypeStruct((d, 4 * real), f32), jax.ShapeDtypeStruct((d, d), f32)),
        grid_spec=pltpu.PrefetchScalarGridSpec(
            num_scalar_prefetch=1, grid=(d // lanes,),
            in_specs=[pl.BlockSpec((a.shape[0], rows, lanes), lambda i, o: (0, 0, i)) for a in arrays],
            out_specs=(pl.BlockSpec((lanes, 4 * real), lambda i, o: (i, 0)), pl.BlockSpec((d, lanes), lambda i, o: (0, i))),
            scratch_shapes=[pltpu.VMEM((4, high, lanes), f32)],
        ),
        compiler_params=pltpu.CompilerParams(vmem_limit_bytes=60 * 2**20),
        name="fill_attn",
    )(own, *arrays)


def on_device(tokens, lengths, w_qkv, b_qkv, w_out, b_out, w_in, b_in, w_down, b_down,
              norm1_gain, norm1_bias, norm2_gain, norm2_bias, cotangent):
    rows, span, d = tokens.shape
    ff = w_in.shape[1]
    head = lax.axis_index("head")
    dp = lax.axis_index("dp")
    x, c = head // 2, head % 2
    y, z = dp % 2, dp // 2
    nz = lax.axis_size("dp") // 2
    own = jnp.stack([x, c, y, z]).astype(jnp.int32)
    row_len = 4 * span
    hd = HEADS // 4 * HW
    flat = lambda a: a.reshape(-1, d)

    gpar = swap(cotangent, "head", 1)
    par = swap(tokens, "head", 1)
    far = swap(tokens, "head", 2)
    gfar = swap(cotangent, "head", 2)
    go, gp = flat(cotangent), flat(gpar)
    xo, xp = flat(tokens), flat(par)
    small = [b_in, b_qkv, b_out, norm1_gain, norm1_bias, norm2_gain, norm2_bias, b_down]
    vecs = gather_vectors(small, d)

    o0, h0, *u0, gb0 = mlp(own, 0, xo, xp, go, gp, w_in, w_down, vecs, nz)
    far, o0, u0, lengths = tie(far, o0, u0, lengths)

    u0r = [swap(u0[1], "dp", 1), swap(u0[3], "dp", 1)]
    farpar = swap(far, "head", 1)
    m_out, m_e, *u1, gb1, ln2 = mlp(own, 1, xo, xp, go, gp, w_in, w_down, vecs, nz, (o0, h0))
    farpar, gfar, u0r, m_out, m_e, u1, lengths = tie(farpar, gfar, u0r, m_out, m_e, u1, lengths)

    gfarpar = swap(gfar, "head", 1)
    u1r = [swap(u1[1], "dp", 1), swap(u1[2], "head", 2), hop(u1[3], 1, 2)]
    u0s, u0 = add(u0[2], u0r[1]), add(u0[0], u0r[0])
    u0r = swap(u0s, "head", 2)
    cos, sin, start = tables(lengths, row_len)
    gfarpar, cos, sin, start = tie(gfarpar, cos, sin, start)
    xs = (tokens, par, far, farpar)
    gs = (cotangent, gpar, gfar, gfarpar)
    me = m_e.reshape(2, rows, span, d)

    def attend(r, w, state, held):
        return attention(own, r, 1, r == rows - 1, xs, gs, w, w_out, vecs, cos, sin, start, me, state, held, (gb0, gb1, ln2), nz)

    *held, gw, gb, ln = attend(0, w_qkv, None, None)
    u0r, u1r, held, gw, gb, ln = tie(u0r, u1r, held, gw, gb, ln)

    u = jnp.stack([add(u0, u0r), total(u1[0], u1r)], axis=1)
    uz = cross(u, nz)
    *held, gw, gb, ln = attend(1, w_qkv, (gw, gb, ln), held)
    uz, held, gw, gb, ln = tie(uz, held, gw, gb, ln)

    whole = lax.all_gather(total(u[0], uz), ("dp", "head"))
    ctx, ctxs, e, es, qk, qs, v = attend(2, w_qkv, (gw, gb, ln), held)
    ctx, ctxs, e, es, qk, qs, v = tie(ctx, ctxs, e, es, qk, qs, v)

    qr = swap(qs, "dp", 1)
    ctxr = swap(ctxs, "head", 2)
    er = swap(es, "head", 1)
    v1 = swap(v, "dp", 2)
    ef = add(e[1], er[1])
    qr, er, v1, ef = tie(qr, er, v1, ef)

    q = add(qk, qr)
    qr = cross(q, nz)
    ex = swap(ef, "head", 2)
    v = v + v1
    v1 = swap(v, "head", 1)
    qr, v1, ctxr = tie(qr, v1, ctxr)

    q = gather_z(total(q[0], qr), nz)
    v = v + v1
    v1 = swap(v, "head", 2)
    keep, send = project(own, ctx, ctxr, w_out, m_out.reshape(2, rows * span, d))
    q, v1, keep, send, ex = tie(q, v1, keep, send, ex)

    zq = jnp.stack(q)
    xq = swap(zq, "head", 2)
    yq = swap(zq, "dp", 1)
    cz = swap(zq, "head", 1)
    outr = swap(send, "head", 1)
    v = v + v1
    bit = 4
    while bit < 2 * nz:
        v = v + swap(v, "dp", bit)
        bit *= 2
    es = e[0].astype(f32) + er[0].astype(f32) + ex.astype(f32)
    n, rho = norm_parts(tokens.astype(f32))
    dx = rho * (es - jnp.mean(es, -1, keepdims=True) - n * jnp.mean(es * n, -1, keepdims=True))
    grad_tokens = (cotangent.astype(f32) + dx).astype(bf)
    shape = (rows, span, d)
    output = (tokens.astype(f32) + keep.astype(f32).reshape(shape) + outr.astype(f32).reshape(shape)
              + (b_out.astype(f32) + b_down.astype(f32))).astype(bf)
    grad_w_in, grad_w_down = fill_mlp(whole.reshape((2 * nz, 4) + whole.shape[1:]))
    xq, yq, cz, v, output, grad_tokens, grad_w_in, grad_w_down = tie(xq, yq, cz, v, output, grad_tokens, grad_w_in, grad_w_down)

    d0 = swap(yq[:nz // 2], "head", 2)
    d1 = swap(xq[nz // 2:], "dp", 1)
    cx, cy = swap(xq, "head", 1), swap(yq, "head", 1)
    v = v + swap(v, "dp", 1)
    d0, d1, cx, cy, v = tie(d0, d1, cx, cy, v)

    c0, c1 = swap(d0, "head", 1), swap(d1, "head", 1)
    parts = (v[4:8, :3 * hd].reshape(-1), v[0:4].reshape(-1), v[8], v[9], v[10], v[11], v[12])
    c0, c1, parts = tie(c0, c1, parts)
    grad_w_qkv, grad_w_out = fill_attn(own, (zq, xq, yq, d0, d1, cz, cx, cy, c0, c1), 3 * hd)

    return (output, grad_tokens, grad_w_qkv, parts[0], grad_w_out, parts[2], grad_w_in, parts[1],
            grad_w_down, parts[2], *parts[3:])


def solution(mesh):
    split = P("dp", "head", None)
    return jax.shard_map(
        on_device, mesh=mesh,
        in_specs=(split, P("dp", None)) + (P(),) * 12 + (split,),
        out_specs=(split, split) + (P(),) * 12,
        check_vma=False,
    )
```

```python
import math, functools
import jax
import jax.numpy as jnp
from jax import lax
from jax.experimental import pallas as pl
from jax.experimental.pallas import tpu as pltpu

bf = jnp.bfloat16
f32 = jnp.float32
NN = (((1,), (0,)), ((), ()))
NT = (((1,), (1,)), ((), ()))
TN = (((0,), (0,)), ((), ()))


def mm(a, b, dims=NN):
    return lax.dot_general(a, b, dims, preferred_element_type=f32)


def norm_parts(x):
    center = x - jnp.mean(x, axis=-1, keepdims=True)
    rho = lax.rsqrt(jnp.mean(center * center, axis=-1, keepdims=True) + 1e-5)
    return center * rho, rho


def normal_cdf(x):
    bell = jnp.exp(-0.5 * x * x)
    t = 1.0 / (1.0 + (0.3275911 * math.sqrt(0.5)) * jnp.abs(x))
    poly = t * (0.127414796 + t * (-0.142248368 + t * (0.7107068705 + t * (-0.7265760135 + t * 0.5307027145))))
    tail = poly * bell
    return jnp.where(x >= 0, 1.0 - tail, tail), bell


def put_quarters(acc, kind, refs, x, y, z):
    nz, rows = refs[0].shape[0], refs[0].shape[1]
    for hy in range(2):
        for at, ref in enumerate(refs):
            jx, jy = at // 2, at % 2

            @pl.when(((x ^ kind) == jx) & ((y ^ hy) == jy))
            def _():
                for hz in range(nz):
                    row = (hz * 2 + hy) * rows
                    ref[hz ^ z] = acc[row:row + rows, :].astype(bf)


def put_halves(acc, half, keep_ref, send_ref, y, z):
    nz, rows = keep_ref.shape[0], keep_ref.shape[1]
    for hy in range(2):
        for ref, stays in ((keep_ref, True), (send_ref, False)):
            @pl.when((y == hy) == stays)
            def _():
                for hz in range(nz):
                    at = hy * half + hz * rows
                    ref[hz ^ z] = acc[at:at + rows, :].astype(bf)


B_IN, B_QKV, B_LAST, GAIN1, BIAS1, GAIN2, BIAS2, VECS = 0, 4, 7, 8, 9, 10, 11, 16


def vector(vec_ref, k, d, count=1):
    return jnp.concatenate([vec_ref[pl.ds(k + i, 1), :] for i in range(count)], axis=1)


def mlp_body(first, own_ref, xo_ref, xp_ref, go_ref, gp_ref, wi_ref, wd_ref, vec_ref, *rest):
    if first:
        out_ref, dh_ref, g0_ref, g1_ref, g2_ref, g3_ref, gbi_ref, *rest = rest
    else:
        outp_ref, dhp_ref, out_ref, e_ref, g0_ref, g1_ref, g2_ref, g3_ref, gbi_ref, ln_ref, n_s, *rest = rest
    h_s, ht_s, g_s, gwi_s, gwd_s = rest
    i, ni = pl.program_id(0), pl.num_programs(0)
    d = xo_ref.shape[1]
    gain = vector(vec_ref, GAIN2, d)

    def start(x_ref, g_ref):
        n, _ = norm_parts(x_ref[...].astype(f32))
        h = (n * gain + vector(vec_ref, BIAS2, d)).astype(bf)
        if not first:
            n_s[...] = n
        h_s[...] = h
        ht_s[...] = h.T
        g_s[...] = g_ref[...]

    @pl.when(i == 0)
    def _():
        start(xo_ref, go_ref)

    @pl.when(i == 1)
    def _():
        start(xp_ref, gp_ref)

    unit = 0 if first else 1
    pre = mm(h_s[...], wi_ref[...]) + vector(vec_ref, B_IN + own_ref[1] * 2 + unit, d)
    d_act = mm(g_s[...], wd_ref[...], NT)
    cdf, bell = normal_cdf(pre)
    act = (pre * cdf).astype(bf)
    slope = cdf + pre * bell * (1.0 / math.sqrt(2.0 * math.pi))
    d_pre = (d_act * slope).astype(bf)
    out = mm(act, wd_ref[...])
    dh = mm(d_pre, wi_ref[...], NT)
    gwi = mm(ht_s[...], d_pre)
    gwd = mm(act.T, g_s[...])
    gbi = jnp.sum(d_pre.astype(f32), axis=0, keepdims=True)

    @pl.when(i == 0)
    def _():
        gwi_s[...] = gwi
        gwd_s[...] = gwd
        gbi_ref[0:1, :] = gbi
        gbi_ref[1:2, :] = jnp.sum(g_s[...].astype(f32), axis=0, keepdims=True)

    @pl.when(i == ni - 1)
    def _():
        gwi_s[...] += gwi
        gwd_s[...] += gwd
        gbi_ref[0:1, :] += gbi
        x, y, z = own_ref[0], own_ref[2], own_ref[3]
        gw = [g0_ref, g1_ref, g2_ref, g3_ref]
        put_quarters(gwi_s, 0, gw, x, y, z)
        put_quarters(gwd_s, 1, gw, x, y, z)

    if first:
        out_ref[...] = out.astype(bf)
        dh_ref[...] = dh.astype(bf)
    else:
        @pl.when(i == 0)
        def _():
            ln_ref[...] = jnp.zeros_like(ln_ref)

        dh = dh + dhp_ref[...].astype(f32)
        out_ref[...] = (out + outp_ref[...].astype(f32)).astype(bf)
        e_ref[...] = (dh * gain).astype(bf)
        ln_ref[0:1, :] += jnp.sum(dh * n_s[...], axis=0, keepdims=True)
        ln_ref[1:2, :] += jnp.sum(dh, axis=0, keepdims=True)


def mlp(own, unit, xo, xp, go, gp, w_in, w_down, vecs, nz, before=None):
    toks, d = xo.shape
    first = before is None
    rows = d // (2 * nz)
    spec = pl.BlockSpec
    once = lambda *s: spec(s, lambda i, o: (0,) * len(s), pipeline_mode=pl.Buffered(1))
    tile = spec((toks, d), lambda i, o: (i, 0))
    part = lambda o: o[1] * 2 + unit
    shape = jax.ShapeDtypeStruct
    vm = pltpu.VMEM
    ins = [once(toks, d)] * 4 + [spec((d, d), lambda i, o: (0, part(o)), pipeline_mode=pl.Buffered(1)),
                                 spec((d, d), lambda i, o: (part(o), 0), pipeline_mode=pl.Buffered(1)), once(*vecs.shape)]
    args = [own, xo, xp, go, gp, w_in, w_down, vecs]
    outs = [shape((2 * toks, d), bf), shape((2 * toks, d), bf)] + [shape((nz, rows, d), bf)] * 4 + [shape((8, d), f32)]
    ospecs = [tile, tile] + [once(nz, rows, d)] * 4 + [once(8, d)]
    scratch = [vm((toks, d), bf)] * 3 + [vm((d, d), f32)] * 2
    if not first:
        ins += [tile, tile]
        args += list(before)
        outs.append(shape((8, d), f32))
        ospecs.append(once(8, d))
        scratch = [vm((toks, d), f32)] + scratch
    return pl.pallas_call(
        functools.partial(mlp_body, first),
        out_shape=tuple(outs),
        grid_spec=pltpu.PrefetchScalarGridSpec(num_scalar_prefetch=1, grid=(2,), in_specs=ins, out_specs=ospecs, scratch_shapes=scratch),
        compiler_params=pltpu.CompilerParams(vmem_limit_bytes=60 * 2**20),
        cost_estimate=pl.CostEstimate(flops=24 * toks * d * d, bytes_accessed=20 * 2**20, transcendentals=2 * toks * d),
        name="mlp%d" % unit,
    )(*args)


HW = 64
ROT = 16


def rope(u, cos, sin, back):
    t, width = u.shape
    lane = lax.broadcasted_iota(jnp.int32, (t, 128), 1)
    inner = lane % HW
    low = inner < ROT // 2
    outs = []
    for b in range(width // 128):
        v = u[:, b * 128:(b + 1) * 128]
        lo_rot, hi_rot = (2 * b) % 3 != 2, (2 * b + 1) % 3 != 2
        if (2 * b + 1) * HW >= 9 * HW:
            hi_rot = False
        if not (lo_rot or hi_rot):
            outs.append(v)
            continue
        turned = inner < ROT
        if not hi_rot:
            turned = turned & (lane < HW)
        if not lo_rot:
            turned = turned & (lane >= HW)
        up = pltpu.roll(v, 128 - ROT // 2, 1)
        down = pltpu.roll(v, ROT // 2, 1)
        if back:
            swapped = jnp.where(low, up, -down)
        else:
            swapped = jnp.where(low, -up, down)
        outs.append(jnp.where(turned, v * cos + swapped * sin, v))
    return jnp.concatenate(outs, axis=1)


def attn_body(first, last, own_ref, xo_ref, xp_ref, xf_ref, xfp_ref, go_ref, gp_ref, gf_ref, gfp_ref, w0_ref, w1_ref, w2_ref, w3_ref, w4_ref, wo_ref, vec_ref,
              cos_ref, sin_ref, start_ref, me_ref, *rest):
    if not first:
        gwp_ref, gbp_ref, lnp_ref, *rest = rest
        rest = rest[4:]
    if last:
        gb0_ref, gb1_ref, ln2_ref, *rest = rest
    ctx_ref, ctxs_ref, e_ref, es_ref, *rest = rest
    if last:
        keep_ref, send_ref, v_ref, *scratch = rest
        gw_s, gb_ref, ln_ref = scratch[-3:]
    else:
        gw_s, gb_ref, ln_ref, *scratch = rest
    x_s, g_s, nb_s, q_s, k_s, v_s, do_s, o_s, dq_s, dk_s, dv_s, cs_s, b_ref, w_ref = scratch[:14]
    head_at = own_ref[0] * 2 + own_ref[1]
    ch = xo_ref.shape[1]
    row_len = start_ref.shape[2]
    nh = q_s.shape[0]
    nch = row_len // ch
    real = nh * 3 * HW
    d_model = x_s.shape[2]
    gain = vector(vec_ref, GAIN1, d_model)
    bias = vector(vec_ref, BIAS1, d_model)

    @pl.when(pl.program_id(0) == 0)
    def _():
        block = own_ref[1] * 2 + own_ref[0]
        b_ref[...] = jnp.zeros_like(b_ref)
        columns = vector(vec_ref, B_QKV, d_model, 3)
        for b in range(4):
            @pl.when(block == b)
            def _():
                b_ref[:, 0:real] = columns[:, b * real:(b + 1) * real]
        for k, ref in enumerate((w0_ref, w1_ref, w2_ref, w3_ref, w4_ref)):
            w_ref[:, k * 128:(k + 1) * 128] = ref[...]
        if first:
            gw_s[...] = jnp.zeros_like(gw_s)
            gb_ref[...] = jnp.zeros_like(gb_ref)
            ln_ref[...] = jnp.zeros_like(ln_ref)
        else:
            gw_s[...] = gwp_ref[...]
            gb_ref[...] = gbp_ref[...]
            ln_ref[...] = lnp_ref[...]

    width = w_ref.shape[1]
    odd = own_ref[0]
    back_by = (width - HW) * odd
    for t, (ref, rest_value) in enumerate(((cos_ref, 1.0), (sin_ref, 0.0))):
        one = ref[0]
        still = jnp.full((HW - ROT, row_len), rest_value, f32)
        cs_s[t] = jnp.concatenate([one, one, still, one, one, still], axis=0).T
    for p, (ref, ref2) in enumerate(((xo_ref, go_ref), (xp_ref, gp_ref), (xf_ref, gf_ref), (xfp_ref, gfp_ref))):
        x_s[p] = ref[0]
        g_s[p] = ref2[0]

    def project(p, _):
        ci = p ^ head_at
        rows = pl.ds(pl.multiple_of(ci * ch, ch), ch)
        n, _ = norm_parts(x_s[p].astype(f32))
        normed = (n * gain + bias).astype(bf)
        nb_s[rows, :] = normed
        lin = pltpu.roll(mm(normed, w_ref[...]), back_by, 1) + b_ref[...]
        lin = rope(lin, cs_s[0, rows, :], cs_s[1, rows, :], False)
        for h in range(nh):
            q_s[h, rows, :] = (lin[:, h * 192:h * 192 + 64].astype(bf) * bf(0.125))
            k_s[h, rows, :] = lin[:, h * 192 + 64:h * 192 + 128].astype(bf)
            v_s[h, rows, :] = lin[:, h * 192 + 128:h * 192 + 192].astype(bf)
        d_ctx = mm(g_s[p], wo_ref[...], NT).astype(bf)
        for h in range(nh):
            do_s[h, rows, :] = d_ctx[:, h * HW:(h + 1) * HW]
        return 0

    for p in range(nch):
        project(p, 0)
    def head(h, _):
        kt = k_s[h].T
        vt = v_s[h].T
        dot_ = do_s[h].astype(f32).T
        for qb in range(nch):
            k0, kn = qb * ch, (qb + 1) * ch
            qs = slice(k0, kn)
            q = q_s[h, qs, :]
            do = do_s[h, qs, :]
            first = start_ref[0, :, qs]
            kpos = lax.broadcasted_iota(jnp.int32, (ch, ch), 0)
            qpos = lax.broadcasted_iota(jnp.int32, (ch, ch), 1)
            st = []
            top = None
            for kb in range(qb + 1):
                s = mm(k_s[h, kb * ch:(kb + 1) * ch, :], q, NT)
                keep = kpos >= first - kb * ch
                if kb == qb:
                    keep = keep & (kpos <= qpos)
                s = jnp.where(keep, s, -1e9)
                m = jnp.max(s, axis=0, keepdims=True)
                top = m if top is None else jnp.maximum(top, m)
                st.append(s)
            size = None
            for kb in range(qb + 1):
                st[kb] = jnp.exp(st[kb] - top)
                m = jnp.sum(st[kb], axis=0, keepdims=True)
                size = m if size is None else size + m
            inv = 1.0 / size
            ot = None
            for kb in range(qb + 1):
                ks = slice(kb * ch, (kb + 1) * ch)
                st[kb] = st[kb] * inv
                pb = st[kb].astype(bf)
                o = mm(vt[:, ks], pb)
                ot = o if ot is None else ot + o
                dv = mm(pb, do)
                if kb < qb:
                    dv_s[h, ks, :] += dv
                else:
                    dv_s[h, ks, :] = dv
            delta = jnp.sum(ot * dot_[:, qs], axis=0, keepdims=True)
            o_s[h * HW:(h + 1) * HW, qs] = ot.astype(bf)
            dqt = None
            for kb in range(qb + 1):
                ks = slice(kb * ch, (kb + 1) * ch)
                dpt = mm(v_s[h, ks, :], do, NT)
                ds = (st[kb] * (dpt - delta)).astype(bf)
                o = mm(kt[:, ks], ds)
                dqt = o if dqt is None else dqt + o
                dk = mm(ds, q)
                if kb < qb:
                    dk_s[h, ks, :] += dk
                else:
                    dk_s[h, ks, :] = dk
            dq_s[h, qs, :] = dqt.T * 0.125
        return 0

    for hh in range(nh):
        head(hh, 0)

    for p in range(nch):
        rows = pl.ds(pl.multiple_of((p ^ head_at) * ch, ch), ch)
        parts = []
        for h in range(nh):
            parts += [dq_s[h, rows, :], dk_s[h, rows, :], dv_s[h, rows, :]]
        parts.append(jnp.zeros((ch, 64), f32))
        d = jnp.concatenate(parts, axis=1).astype(bf).astype(f32)
        d = rope(d, cs_s[0, rows, :], cs_s[1, rows, :], True)
        placed = pltpu.roll(d, HW * odd, 1).astype(bf)
        d = d.astype(bf)
        gb_ref[...] += jnp.sum(d.astype(f32), axis=0, keepdims=True)
        dn = mm(placed, w_ref[...], NT)
        n, _ = norm_parts(x_s[p].astype(f32))
        ln_ref[0:1, :] += jnp.sum(dn * n, axis=0, keepdims=True)
        ln_ref[1:2, :] += jnp.sum(dn, axis=0, keepdims=True)
        e = dn * gain
        if p < 2:
            e = e + me_ref[p, 0].astype(f32)
        (es_ref if p % 2 else e_ref)[p // 2, 0] = e.astype(bf)
        gw_s[0:real, :] += mm(d.T[0:real], nb_s[rows, :])
        ctx = o_s[:, rows]
        (ctx_ref if p < 2 else ctxs_ref)[p % 2, 0] = ctx
        gw_s[real:, :] += mm(ctx, g_s[p])

    if last:
        @pl.when(pl.program_id(0) == pl.num_programs(0) - 1)
        def _():
            put_halves(gw_s, gw_s.shape[0] // 2, keep_ref, send_ref, own_ref[2], own_ref[3])
            v_ref[...] = jnp.zeros_like(v_ref)
            for u, ref in enumerate((gb0_ref, gb1_ref)):
                v_ref[pl.ds(own_ref[1] * 2 + u, 1), :] = ref[0:1, :]
            v_ref[pl.ds(4 + own_heads(own_ref), 1), 0:real] = gb_ref[:, 0:real]
            v_ref[8:9, :] = gb0_ref[1:2, :]
            v_ref[9:11, :] = ln_ref[0:2, :]
            v_ref[11:13, :] = ln2_ref[0:2, :]


def attention(own, r0, nr, last, xs, gs, w, w_out, vecs, cos, sin, start, me, before, held, sums, nz):
    rows_all, span, d = xs[0].shape
    row_len = start.shape[2]
    hd = w_out.shape[0] // 4
    nh = hd // HW
    real = nh * 3 * HW
    width = real + HW
    high = real + hd
    first = before is None
    spec = pl.BlockSpec
    at_row = lambda *s: spec((1,) + s, lambda i, o: (r0 + i, 0, 0))
    two = lambda *s: spec((2, 1) + s, lambda i, o: (0, r0 + i, 0, 0))
    whole = lambda *s: spec(s, lambda i, o: (0,) * len(s))
    shape = jax.ShapeDtypeStruct
    pieces = (nz, high // (2 * nz), d)
    outs = [shape((2, rows_all, hd, span), bf)] * 2 + [shape((2, rows_all, span, d), bf)] * 2
    ospecs = [two(hd, span)] * 2 + [two(span, d)] * 2
    sum_shapes = [(high, d), (1, width), (8, d)]
    if last:
        outs += [shape(pieces, bf)] * 2 + [shape((16, d), f32)]
        ospecs += [whole(*pieces)] * 2 + [whole(16, d)]
    else:
        outs += [shape(t, f32) for t in sum_shapes]
        ospecs += [whole(*t) for t in sum_shapes]
    heads = lambda dt: pltpu.VMEM((nh, row_len, HW), dt)
    scratch = [pltpu.VMEM((4, span, d), bf)] * 2 + [pltpu.VMEM((row_len, d), bf)] + [heads(bf)] * 4 + [pltpu.VMEM((hd, row_len), bf)] + [heads(f32)] * 3 + [
        pltpu.VMEM((2, row_len, 2 * HW), f32), pltpu.VMEM((1, width), f32), pltpu.VMEM((d, width), bf)]
    window = lambda k: spec((d, 128), lambda i, o: (0, own_heads(o) * real // 128 + k))
    ins = [at_row(span, d)] * 8 + [window(k) for k in range(width // 128)] + [
        spec((hd, d), lambda i, o: (own_heads(o), 0)), whole(*vecs.shape), at_row(*cos.shape[1:]), at_row(*cos.shape[1:]),
        at_row(1, row_len), two(span, d)]
    args = [own, *xs, *gs, *[w] * (width // 128), w_out, vecs, cos, sin, start, me]
    alias = {}
    if not first:
        ins += [whole(*t) for t in sum_shapes]
        args += list(before)
        alias = {len(args) + k: k for k in range(4)}
        ins += [spec(memory_space=pl.ANY)] * 4
        args += list(held)
    if last:
        scratch += [pltpu.VMEM(t, f32) for t in sum_shapes]
        ins += [whole(8, d)] * 3
        args += list(sums)
    return pl.pallas_call(
        functools.partial(attn_body, first, last),
        out_shape=tuple(outs),
        grid_spec=pltpu.PrefetchScalarGridSpec(num_scalar_prefetch=1, grid=(nr,), in_specs=ins, out_specs=ospecs, scratch_shapes=scratch),
        input_output_aliases=alias,
        compiler_params=pltpu.CompilerParams(vmem_limit_bytes=60 * 2**20),
        cost_estimate=pl.CostEstimate(flops=nr * row_len * (8 * d * real + 6 * row_len * hd * 4), bytes_accessed=20 * 2**20, transcendentals=nr * nh * row_len * row_len // 2),
        name="attention%d" % r0,
    )(*args)


def own_heads(own):
    return own[1] * 2 + own[0]


def far_heads(own):
    return own[1] * 2 + 1 - own[0]


def project_body(own_ref, mine_ref, came_ref, wm_ref, wf_ref, mo_ref, keep_ref, send_ref):
    _, nr, _, span = mine_ref.shape
    for r in range(nr):
        rows = slice(r * span, (r + 1) * span)
        for p, out_ref in enumerate((keep_ref, send_ref)):
            out_ref[rows, :] = (mm(mine_ref[p, r], wm_ref[...], TN) + mm(came_ref[p, r], wf_ref[...], TN) + mo_ref[p, rows, :].astype(f32)).astype(bf)


def project(own, mine, came, w_out, m_out):
    _, toks, d = m_out.shape
    hd = mine.shape[2]
    spec = pl.BlockSpec
    whole = lambda *s: spec(s, lambda i, o: (0,) * len(s))
    shape = jax.ShapeDtypeStruct
    return pl.pallas_call(
        project_body,
        out_shape=(shape((toks, d), bf), shape((toks, d), bf)),
        grid_spec=pltpu.PrefetchScalarGridSpec(
            num_scalar_prefetch=1, grid=(1,),
            in_specs=[whole(*mine.shape)] * 2 + [
                spec((hd, d), lambda i, o: (own_heads(o), 0)), spec((hd, d), lambda i, o: (far_heads(o), 0)), whole(2, toks, d)],
            out_specs=[whole(toks, d)] * 2,
        ),
        compiler_params=pltpu.CompilerParams(vmem_limit_bytes=60 * 2**20),
        name="project",
    )(own, mine, came, w_out, w_out, m_out)


from jax.sharding import PartitionSpec as P

HEADS = 12


def swap(x, axis, bit):
    n = lax.axis_size(axis)
    return lax.ppermute(x, axis, [(i, i ^ bit) for i in range(n)])


def add(a, b):
    return (a.astype(f32) + b.astype(f32)).astype(bf)


def tie(*groups):
    return lax.optimization_barrier(groups)


def hop(x, dp_bit, head_bit):
    nd, nh = lax.axis_size("dp"), lax.axis_size("head")
    return lax.ppermute(x, ("dp", "head"), [(i * nh + j, (i ^ dp_bit) * nh + (j ^ head_bit)) for i in range(nd) for j in range(nh)])


def cross(pieces, nz):
    return [swap(pieces[k], "dp", 2 * k) for k in range(1, nz)]


def gather_z(piece, nz):
    return [piece] + [swap(piece, "dp", 2 * k) for k in range(1, nz)]


def total(first, came):
    t = first.astype(f32)
    for c in came:
        t = t + c.astype(f32)
    return t.astype(bf)


def gather_vectors(vectors, d):
    def body(*refs):
        out_ref = refs[-1]
        out_ref[...] = jnp.zeros_like(out_ref)
        at = 0
        for ref in refs[:-1]:
            n = ref.shape[0]
            row = ref[...].astype(f32).reshape(1, n)
            for k in range(n // d):
                out_ref[at + k:at + k + 1, :] = row[:, k * d:(k + 1) * d]
            at += n // d

    vm = pl.BlockSpec(memory_space=pltpu.VMEM)
    return pl.pallas_call(
        body,
        out_shape=jax.ShapeDtypeStruct((VECS, d), f32),
        in_specs=[vm] * len(vectors),
        out_specs=vm,
        compiler_params=pltpu.CompilerParams(vmem_limit_bytes=60 * 2**20),
        name="vectors",
    )(*vectors)


def tables(lengths, row_len):
    pos = jnp.arange(row_len, dtype=jnp.int32)[None, :]
    first_end = lengths[:, 0:1]
    second_end = first_end + lengths[:, 1:2]
    start = jnp.where(pos < first_end, 0, jnp.where(pos < second_end, first_end, second_end))
    half = ROT // 2
    freq = 1.0 / 10000.0 ** (jnp.arange(half, dtype=f32) * 2.0 / ROT)
    angle = (pos - start)[:, None, :].astype(f32) * freq[None, :, None]

    return jnp.cos(angle), jnp.sin(angle), start[:, None, :]


def fill_body(nu, pieces_ref, wi_ref, wd_ref):
    d = pieces_ref.shape[-1]
    for c in range(2):
        for u in range(nu):
            b = c * nu + u
            wi_ref[:, b * d:(b + 1) * d] = pieces_ref[0, c, u].astype(f32)
            wd_ref[b, 0] = pieces_ref[1, c, u].astype(f32)


def fill_mlp(pieces):
    nd, nh, nu, rows, d = pieces.shape
    wi, wd = pl.pallas_call(
        functools.partial(fill_body, nu),
        grid=(nd,),
        out_shape=(jax.ShapeDtypeStruct((nd * rows, 2 * nu * d), f32), jax.ShapeDtypeStruct((2 * nu, nd, rows, d), f32)),
        in_specs=[pl.BlockSpec((None, 2, 2, nu, rows, d), lambda i: (i, 0, 0, 0, 0, 0))],
        out_specs=(pl.BlockSpec((rows, 2 * nu * d), lambda i: (i, 0)), pl.BlockSpec((2 * nu, 1, rows, d), lambda i: (0, i, 0, 0))),
        compiler_params=pltpu.CompilerParams(vmem_limit_bytes=60 * 2**20),
        name="fill_mlp",
    )(pieces.reshape(nd, 2, 2, nu, rows, d))
    return wi, wd.reshape(2 * nu * nd * rows, d)


def fill_attn(own, arrays, real):
    nz, rows, d = arrays[0].shape
    high = 2 * nz * rows
    lanes = 256
    parts = [(0, 0, 0), (1, 0, 0), (0, 1, 0), (1, 1, 0), (1, 1, nz // 2)]

    def body(own_ref, *refs):
        wq_ref, wo_ref, s = refs[10:]
        x, c, y, z = own_ref[0], own_ref[1], own_ref[2], own_ref[3]
        for k in range(10):
            jx, jy, lo = parts[k % 5]
            block = (c ^ (k // 5)) * 2 + (x ^ jx)
            for t in range(refs[k].shape[0]):
                at = pl.multiple_of(((y ^ jy) * nz + (z ^ (lo + t))) * rows, 8)
                s[block, pl.ds(at, rows), :] = refs[k][t].astype(f32)
        for b in range(4):
            wq_ref[:, b * real:(b + 1) * real] = s[b, 0:real].T
            wo_ref[b * (high - real):(b + 1) * (high - real), :] = s[b, real:]

    return pl.pallas_call(
        body,
        out_shape=(jax.ShapeDtypeStruct((d, 4 * real), f32), jax.ShapeDtypeStruct((d, d), f32)),
        grid_spec=pltpu.PrefetchScalarGridSpec(
            num_scalar_prefetch=1, grid=(d // lanes,),
            in_specs=[pl.BlockSpec((a.shape[0], rows, lanes), lambda i, o: (0, 0, i)) for a in arrays],
            out_specs=(pl.BlockSpec((lanes, 4 * real), lambda i, o: (i, 0)), pl.BlockSpec((d, lanes), lambda i, o: (0, i))),
            scratch_shapes=[pltpu.VMEM((4, high, lanes), f32)],
        ),
        compiler_params=pltpu.CompilerParams(vmem_limit_bytes=60 * 2**20),
        name="fill_attn",
    )(own, *arrays)


def on_device(tokens, lengths, w_qkv, b_qkv, w_out, b_out, w_in, b_in, w_down, b_down,
              norm1_gain, norm1_bias, norm2_gain, norm2_bias, cotangent):
    rows, span, d = tokens.shape
    ff = w_in.shape[1]
    head = lax.axis_index("head")
    dp = lax.axis_index("dp")
    x, c = head // 2, head % 2
    y, z = dp % 2, dp // 2
    nz = lax.axis_size("dp") // 2
    own = jnp.stack([x, c, y, z]).astype(jnp.int32)
    row_len = 4 * span
    hd = HEADS // 4 * HW
    flat = lambda a: a.reshape(-1, d)

    gpar = swap(cotangent, "head", 1)
    par = swap(tokens, "head", 1)
    far = swap(tokens, "head", 2)
    gfar = swap(cotangent, "head", 2)
    go, gp = flat(cotangent), flat(gpar)
    xo, xp = flat(tokens), flat(par)
    small = [b_in, b_qkv, b_out, norm1_gain, norm1_bias, norm2_gain, norm2_bias, b_down]
    vecs = gather_vectors(small, d)

    o0, h0, *u0, gb0 = mlp(own, 0, xo, xp, go, gp, w_in, w_down, vecs, nz)
    far, o0, u0, lengths = tie(far, o0, u0, lengths)

    u0r = [swap(u0[1], "dp", 1), swap(u0[3], "dp", 1)]
    farpar = swap(far, "head", 1)
    m_out, m_e, *u1, gb1, ln2 = mlp(own, 1, xo, xp, go, gp, w_in, w_down, vecs, nz, (o0, h0))
    farpar, gfar, u0r, m_out, m_e, u1, lengths = tie(farpar, gfar, u0r, m_out, m_e, u1, lengths)

    gfarpar = swap(gfar, "head", 1)
    u1r = [swap(u1[1], "dp", 1), swap(u1[2], "head", 2), hop(u1[3], 1, 2)]
    u0s, u0 = add(u0[2], u0r[1]), add(u0[0], u0r[0])
    u0r = swap(u0s, "head", 2)
    cos, sin, start = tables(lengths, row_len)
    gfarpar, cos, sin, start = tie(gfarpar, cos, sin, start)
    xs = (tokens, par, far, farpar)
    gs = (cotangent, gpar, gfar, gfarpar)
    me = m_e.reshape(2, rows, span, d)

    def attend(r, w, state, held):
        return attention(own, r, 1, r == rows - 1, xs, gs, w, w_out, vecs, cos, sin, start, me, state, held, (gb0, gb1, ln2), nz)

    *held, gw, gb, ln = attend(0, w_qkv, None, None)
    u0r, u1r, held, gw, gb, ln = tie(u0r, u1r, held, gw, gb, ln)

    u = jnp.stack([add(u0, u0r), total(u1[0], u1r)], axis=1)
    uz = cross(u, nz)
    *held, gw, gb, ln = attend(1, w_qkv, (gw, gb, ln), held)
    uz, held, gw, gb, ln = tie(uz, held, gw, gb, ln)

    whole = lax.all_gather(total(u[0], uz), ("dp", "head"))
    ctx, ctxs, e, es, qk, qs, v = attend(2, w_qkv, (gw, gb, ln), held)
    ctx, ctxs, e, es, qk, qs, v = tie(ctx, ctxs, e, es, qk, qs, v)

    qr = swap(qs, "dp", 1)
    ctxr = swap(ctxs, "head", 2)
    er = swap(es, "head", 1)
    v1 = swap(v, "dp", 2)
    ef = add(e[1], er[1])
    qr, er, v1, ef = tie(qr, er, v1, ef)

    q = add(qk, qr)
    qr = cross(q, nz)
    ex = swap(ef, "head", 2)
    v = v + v1
    v1 = swap(v, "head", 1)
    qr, v1, ctxr = tie(qr, v1, ctxr)

    q = gather_z(total(q[0], qr), nz)
    v = v + v1
    v1 = swap(v, "head", 2)
    keep, send = project(own, ctx, ctxr, w_out, m_out.reshape(2, rows * span, d))
    q, v1, keep, send, ex = tie(q, v1, keep, send, ex)

    zq = jnp.stack(q)
    xq = swap(zq, "head", 2)
    yq = swap(zq, "dp", 1)
    cz = swap(zq, "head", 1)
    outr = swap(send, "head", 1)
    v = v + v1
    bit = 4
    while bit < 2 * nz:
        v = v + swap(v, "dp", bit)
        bit *= 2
    grad_w_in, grad_w_down = fill_mlp(whole.reshape((2 * nz, 4) + whole.shape[1:]))
    xq, yq, cz, v, outr, grad_w_in, grad_w_down = tie(xq, yq, cz, v, outr, grad_w_in, grad_w_down)

    d0 = swap(yq[:nz // 2], "head", 2)
    d1 = swap(xq[nz // 2:], "dp", 1)
    cx, cy = swap(xq, "head", 1), swap(yq, "head", 1)
    v = v + swap(v, "dp", 1)
    es = e[0].astype(f32) + er[0].astype(f32) + ex.astype(f32)
    n, rho = norm_parts(tokens.astype(f32))
    dx = rho * (es - jnp.mean(es, -1, keepdims=True) - n * jnp.mean(es * n, -1, keepdims=True))
    grad_tokens = (cotangent.astype(f32) + dx).astype(bf)
    shape = (rows, span, d)
    output = (tokens.astype(f32) + keep.astype(f32).reshape(shape) + outr.astype(f32).reshape(shape)
              + (b_out.astype(f32) + b_down.astype(f32))).astype(bf)
    d0, d1, cx, cy, v, output, grad_tokens = tie(d0, d1, cx, cy, v, output, grad_tokens)

    c0, c1 = swap(d0, "head", 1), swap(d1, "head", 1)
    parts = (v[4:8, :3 * hd].reshape(-1), v[0:4].reshape(-1), v[8], v[9], v[10], v[11], v[12])
    c0, c1, parts = tie(c0, c1, parts)
    grad_w_qkv, grad_w_out = fill_attn(own, (zq, xq, yq, d0, d1, cz, cx, cy, c0, c1), 3 * hd)

    return (output, grad_tokens, grad_w_qkv, parts[0], grad_w_out, parts[2], grad_w_in, parts[1],
            grad_w_down, parts[2], *parts[3:])


def solution(mesh):
    split = P("dp", "head", None)
    return jax.shard_map(
        on_device, mesh=mesh,
        in_specs=(split, P("dp", None)) + (P(),) * 12 + (split,),
        out_specs=(split, split) + (P(),) * 12,
        check_vma=False,
    )
```
